256 devices in a mesh: pre: 16 (over y, x), seq: 8 (over z), dec: 2 (over core).
Axes of the slice: x: 4, y: 4, z: 8, core: 2. Of those that a mesh axis runs over, the one named last changes fastest.
Arguments:
- block_pool: bfloat16 [16, 8, 2, 80, 128, 576], P('pre', 'seq', 'dec'), may hold values from -6 to 6
- block_table: int32 [16, 8, 2, 128], P('pre', 'seq', 'dec'), may hold values from 0 to 79, as said below
- lengths: int32 [16, 16], P('pre'), may hold values from 1 to 16384, as said below
- destination: int32 [16, 16], P('pre'), may hold values from 0 to 15, each once within a row
- query_latent: bfloat16 [16, 16, 2, 128, 576], P('pre', None, None, ('seq', 'dec'))
- new_latent: bfloat16 [16, 16, 2, 576], P('pre')
- value_proj: bfloat16 [128, 512, 128], P(('seq', 'dec')), may hold values from -0.25 to 0.25
Outputs:
- attended: bfloat16 [16, 16, 2, 16384], P('pre', None, None, ('seq', 'dec'))
The draws below stay inside these ranges and needn't reach their ends.
Inputs may be any that keep to these rules, and one draw needn't show every extreme that they name: `block_table`: on each device, the slots of a request that hold positions below its length name distinct pool blocks; other slots name any block. `destination`: each prefill device's row names every code 0 to 15 once. Each prefill device's lengths sum to 131072, and one of them is 16384.
All inputs are finite; a program needn't handle non-finite values.
Results may differ from the reference program's by a relative error of at most 0.0051.
Values may be sent and summed in bfloat16 or wider, within the bound.
No kernel may reach another device: no remote copies, remote signals or barrier semaphores. Data moves between devices by JAX's collectives and lax.ppermute only.
A program may use at most 192 MiB of HBM per device.

```python
import jax
import jax.numpy as jnp
from jax import lax

DLAT = 512
DROPE = 64
HEADS = 128
DV = 128
BLOCK = 128
STEPS = 2
SLOTS = 8
RPP = 1
KV = 576
REQ_DEV = 16
POOL = 80
NSPLIT = 16
MAXLEN = 16384
N_PRE = 16
N_SEQ = 8
N_DEC = 2


def shared_lengths(key):
    key = jax.random.fold_in(key, 40)
    first_key, second_key = jax.random.split(key)
    shares = jax.random.randint(first_key, (N_PRE, REQ_DEV), 2, 5)
    longest = jax.random.randint(second_key, (N_PRE,), 0, REQ_DEV)
    request_ids = jnp.arange(REQ_DEV, dtype=jnp.int32)
    is_longest = request_ids[None, :] == longest[:, None]
    remaining = REQ_DEV * MAXLEN // 2 - MAXLEN
    used_shares = jnp.where(is_longest, 0, shares)
    share_total = jnp.sum(used_shares, axis=1, keepdims=True)
    portion = used_shares * remaining // share_total
    leftover = remaining - jnp.sum(portion, axis=1)
    smallest = jnp.argmin(jnp.where(is_longest, 100, shares), axis=1).astype(jnp.int32)
    portion = portion + jnp.where(request_ids[None, :] == smallest[:, None], leftover[:, None], 0)
    return jnp.where(is_longest, MAXLEN, portion).astype(jnp.int32)


def draw_lengths(key, part):
    return shared_lengths(key)


def draw_block_table(key, part):
    request_lengths = shared_lengths(key)
    key = jax.random.fold_in(key, 41)
    split_ids = jnp.arange(NSPLIT, dtype=jnp.int32)
    stride = NSPLIT * BLOCK
    counts = (request_lengths[:, None, :] - split_ids[None, :, None] * BLOCK + stride - 1) // stride
    counts = jnp.maximum(counts, 0)
    before = jnp.cumsum(counts, axis=2) - counts
    used_total = jnp.sum(counts, axis=2, keepdims=True)
    slot_ids = jnp.arange(SLOTS, dtype=jnp.int32)
    request_ids = jnp.arange(REQ_DEV, dtype=jnp.int32)
    used = slot_ids[None, None, None, :] < counts[..., None]
    used_rank = before[..., None] + slot_ids[None, None, None, :]
    spare_rank = used_total[..., None] + request_ids[None, None, :, None] * SLOTS - before[..., None] + slot_ids[None, None, None, :] - counts[..., None]
    rank = jnp.where(used, used_rank, spare_rank) % POOL
    keys = jax.random.split(key, N_PRE * NSPLIT)
    orders = jax.vmap(lambda one: jax.random.permutation(one, POOL))(keys).reshape(N_PRE, NSPLIT, POOL).astype(jnp.int32)
    flat_rank = rank.reshape(N_PRE, NSPLIT, REQ_DEV * SLOTS)
    table = jnp.take_along_axis(orders, flat_rank, axis=2)
    return table.reshape(N_PRE, N_SEQ, N_DEC, REQ_DEV * SLOTS).astype(jnp.int32)


def fresh_base(key):
    return jnp.clip(jax.random.normal(key, (N_PRE, REQ_DEV, STEPS, DLAT + DROPE), jnp.float32), -4.0, 4.0)


def draw_new_latent(key, part):
    base = fresh_base(key)
    return base.astype(jnp.bfloat16)


def draw_query_latent(key, part):
    key = jax.random.fold_in(key, 22)
    drawn = 0.5 * jnp.clip(jax.random.normal(key, (N_PRE, REQ_DEV, STEPS, HEADS, DLAT + DROPE), jnp.float32), -4.0, 4.0)
    return drawn.astype(jnp.bfloat16)


def block_scale(own_key, dims, pieces, low, top_value):
    factor_of = 1.0
    for axis_at, parts in pieces:
        steps = jax.random.uniform(jax.random.fold_in(jax.random.fold_in(own_key, 6), axis_at), (parts,), jnp.float32, low / len(pieces), top_value / len(pieces))
        factor_of = factor_of * jnp.repeat(jnp.exp(steps), dims[axis_at] // parts).reshape((-1,) + (1,) * (len(dims) - 1 - axis_at))
    return factor_of


def bell_draw(stream_key, dims, spread, most, cuts=(), kind=jnp.bfloat16):
    values = jax.random.normal(stream_key, dims, jnp.float32) * spread
    if len(cuts) > 0:
        values = block_scale(stream_key, dims, cuts, -0.22, 0.18) * values
    return jnp.clip(values, min=-most, max=most).astype(kind)


def setup_inputs(seed: int = 0) -> dict:
    arg_keys = jax.random.split(jax.random.key(seed), 8)
    block_pool = bell_draw(arg_keys[0], (N_PRE, N_SEQ, N_DEC, POOL, BLOCK, KV), 1.0, 6.0, ((0, 16), (1, 8), (2, 2)))
    block_table = draw_block_table(jax.random.fold_in(arg_keys[7], 71), 0)
    lengths = draw_lengths(jax.random.fold_in(arg_keys[7], 71), 0)
    destination = jax.vmap(lambda own: jax.random.permutation(own, REQ_DEV))(jax.random.split(arg_keys[3], N_PRE)).reshape((N_PRE, REQ_DEV)).astype(jnp.int32)
    query_latent = draw_query_latent(jax.random.fold_in(arg_keys[7], 71), 0)
    new_latent = draw_new_latent(jax.random.fold_in(arg_keys[7], 71), 0)
    value_proj = bell_draw(arg_keys[6], (HEADS, DLAT, DV), DLAT ** -0.5, 0.25, ((0, 16),))
    return {"block_pool": block_pool, "block_table": block_table, "lengths": lengths, "destination": destination, "query_latent": query_latent, "new_latent": new_latent, "value_proj": value_proj}


score_scale = 192.0 ** -0.5


def one_request(query_rows, new_keys, cached, length):
    scores = jnp.dot(query_rows, cached.T, preferred_element_type=jnp.float32) * score_scale
    usable = jnp.arange(MAXLEN, dtype=jnp.int32) < length
    scores = jnp.where(usable[None, :], scores, -jnp.inf)
    new_scores = jnp.dot(query_rows, new_keys.T, preferred_element_type=jnp.float32) * score_scale
    row_step = jnp.arange(STEPS * HEADS, dtype=jnp.int32) // HEADS
    causal = jnp.arange(STEPS, dtype=jnp.int32)[None, :] <= row_step[:, None]
    new_scores = jnp.where(causal, new_scores, -jnp.inf)
    top_row = jnp.maximum(jnp.max(scores, axis=-1), jnp.max(new_scores, axis=-1))
    weights = jnp.exp(scores - top_row[:, None])
    new_weights = jnp.exp(new_scores - top_row[:, None])
    denominator = jnp.sum(weights, axis=-1) + jnp.sum(new_weights, axis=-1)
    numerator = jnp.dot(weights.astype(jnp.bfloat16), cached[:, :DLAT], preferred_element_type=jnp.float32)
    numerator = numerator + jnp.dot(new_weights.astype(jnp.bfloat16), new_keys[:, :DLAT], preferred_element_type=jnp.float32)
    latent = (numerator / denominator[:, None]).astype(jnp.bfloat16)
    return latent.reshape(STEPS, HEADS, DLAT)


def reference(block_pool, block_table, lengths, destination, query_latent, new_latent, value_proj):
    dest_dev = destination // RPP
    dest_slot = jnp.arange(N_PRE, dtype=jnp.int32)[:, None] * RPP + destination % RPP
    query_pref = query_latent[dest_dev, dest_slot].reshape(N_PRE * REQ_DEV, STEPS * HEADS, KV)
    new_pref = new_latent[dest_dev, dest_slot].reshape(N_PRE * REQ_DEV, STEPS, KV)
    part_pool = block_pool.reshape(N_PRE, NSPLIT, POOL, BLOCK, KV)
    part_table = block_table.reshape(N_PRE, NSPLIT, REQ_DEV, SLOTS)
    split_ids = jnp.arange(NSPLIT, dtype=jnp.int32)[:, None]

    def per_request(items):
        flat_index, query_rows, new_keys, length = items
        owner = flat_index // REQ_DEV
        local = flat_index % REQ_DEV
        rows_used = part_table[owner, :, local, :]
        picked = part_pool[owner, split_ids, rows_used]
        cached = jnp.transpose(picked, (1, 0, 2, 3)).reshape(MAXLEN, KV)
        return one_request(query_rows, new_keys, cached, length)

    flat_ids = jnp.arange(N_PRE * REQ_DEV, dtype=jnp.int32)
    latents = lax.map(per_request, (flat_ids, query_pref, new_pref, lengths.reshape(N_PRE * REQ_DEV)))
    values = jnp.einsum("nshc,hcv->nshv", latents.astype(jnp.float32), value_proj.astype(jnp.float32))
    values = values.astype(jnp.bfloat16).reshape(N_PRE, REQ_DEV, STEPS, HEADS * DV)
    output = jnp.zeros((N_PRE, REQ_DEV, STEPS, HEADS * DV), jnp.bfloat16)
    return output.at[dest_dev, dest_slot].set(values)
```

```python
import functools

import jax
import jax.numpy as jnp
from jax import lax
from jax.experimental import pallas as pl
from jax.experimental.pallas import tpu as pltpu
from jax.sharding import PartitionSpec as P

score_scale = 192.0 ** (-0.5) * 1.4426950408889634
EMPTY = -(2.0**127)
F32 = jnp.float32
BF16 = jnp.bfloat16
MIB = 1024 * 1024
GROUP = 4


def pack_stat(stat):
    high = stat.astype(BF16)
    rest = stat - high.astype(F32)
    mid = rest.astype(BF16)
    low = (rest - mid.astype(F32)).astype(BF16)
    return high, mid, low


def read_stat(ref):
    requests = ref.shape[0] - 1
    parts = [ref[requests, :, i * 128 : (i + 1) * 128].astype(F32) for i in range(3)]
    return parts[0] + parts[1] + parts[2]


def write_stat(ref, stat):
    requests = ref.shape[0] - 1
    for i, part in enumerate(pack_stat(stat)):
        ref[requests, :, i * 128 : (i + 1) * 128] = part
    used = 3 * 128
    if ref.shape[2] > used:
        ref[requests, :, used:] = jnp.zeros((ref.shape[1], ref.shape[2] - used), BF16)


def plan_kernel(split_count, block, dest_ref, len_ref, table_ref, split_ref, out_ref, next_ref):
    requests = dest_ref.shape[1]
    slots = table_ref.shape[3] // requests
    split = split_ref[0]
    counts = []
    for i in range(requests):
        total = lax.div(len_ref[0, i] + (block - 1), block)
        counts.append(lax.div(total - split + (split_count - 1), split_count))
    pairs = [lax.div(count + 1, 2) for count in counts]
    for c in range(slots // 2 + 1):
        longer = [(p > c).astype(jnp.int32) for p in pairs]
        next_ref[c] = functools.reduce(jnp.add, longer)
    for i in range(requests):
        at = next_ref[pairs[i]]
        next_ref[pairs[i]] = at + 1
        start = (counts[i] - 1) * split_count + split
        used = (counts[i] - 1) * block + jnp.minimum(block, len_ref[0, i] - start * block)
        out_ref[at, 0] = dest_ref[0, i]
        out_ref[at, 1] = pairs[i]
        out_ref[at, 2] = jnp.where(counts[i] > 0, used, 0)
        for j in range(slots):
            out_ref[at, 3 + j] = table_ref[0, 0, 0, i * slots + j]


def attention_kernel(n_pieces, plan_ref, *refs):
    q_refs = refs[:n_pieces]
    pool_ref = refs[n_pieces]
    o_refs = refs[n_pieces + 1 : 2 * n_pieces + 1]
    kbuf, stat_ref, sems = refs[2 * n_pieces + 1 :]
    requests, rows, _ = q_refs[0].shape
    slots = plan_ref.shape[1] - 3
    block = pool_ref.shape[2]
    latent = o_refs[0].shape[2]
    groups = requests // GROUP

    def each(g, act):
        pairs = plan_ref[g * GROUP, 1]
        half = lax.rem(g, 2)
        for m in range(GROUP):
            for j in range(slots):

                @pl.when(j // 2 < pairs)
                def _():
                    act(
                        pltpu.make_async_copy(
                            pool_ref.at[plan_ref[g * GROUP + m, 3 + j]],
                            kbuf.at[half, m, j],
                            sems.at[half, m, j],
                        )
                    )

    each(0, lambda c: c.start())
    stat_ref[...] = jnp.zeros_like(stat_ref)
    lane = lax.broadcasted_iota(jnp.int32, stat_ref.shape, 1)
    pair = 2 * block
    column = lax.broadcasted_iota(jnp.int32, (1, pair), 1)

    def compute(g, pairs):
        half = lax.rem(g, 2)
        whos = [plan_ref[g * GROUP + m, 0] for m in range(GROUP)]
        keys, scores, tops = [], [], []
        for m, who in enumerate(whos):
            used = plan_ref[g * GROUP + m, 2]
            q = jnp.concatenate([ref[who] for ref in q_refs], axis=0)
            keys.append(
                [
                    jnp.concatenate([kbuf[half, m, 2 * c], kbuf[half, m, 2 * c + 1]], axis=1)
                    for c in range(pairs)
                ]
            )
            row = []
            for c in range(pairs):
                s = jnp.dot(q, keys[m][c], preferred_element_type=F32) * score_scale
                row.append(jnp.where(column < used - c * pair, s, -jnp.inf))
            scores.append(row)
        for row in scores:
            top = functools.reduce(jnp.maximum, row)
            tops.append(jnp.maximum(jnp.max(top, axis=1, keepdims=True), EMPTY))
        for m, who in enumerate(whos):
            total, out = None, None
            for c in range(pairs):
                e = jnp.exp2(scores[m][c] - tops[m])
                total = e if total is None else total + e
                part = lax.dot_general(
                    e.astype(BF16),
                    keys[m][c][:latent],
                    (((1,), (1,)), ((), ())),
                    preferred_element_type=F32,
                )
                out = part if out is None else out + part
            total = jnp.sum(total, axis=1, keepdims=True)
            some = total > 0
            out = (out * jnp.where(some, 1.0 / total, 0.0)).astype(BF16)
            for n, ref in enumerate(o_refs):
                ref[who] = out[n * rows : (n + 1) * rows]
            stat = jnp.where(some, tops[m] + jnp.log2(total), EMPTY)
            stat_ref[...] = jnp.where(lane == who, stat, stat_ref[...])

    def step(g, carry):
        @pl.when(g + 1 < groups)
        def _():
            each(g + 1, lambda c: c.start())

        each(g, lambda c: c.wait())
        pairs_here = plan_ref[g * GROUP, 1]
        for pairs in range(1, slots // 2 + 1):

            @pl.when(pairs_here == pairs)
            def _():
                compute(g, pairs)

        @pl.when(pairs_here == 0)
        def _():
            for m in range(GROUP):
                who = plan_ref[g * GROUP + m, 0]
                for ref in o_refs:
                    ref[who] = jnp.zeros((rows, latent), BF16)
                stat_ref[...] = jnp.where(lane == who, EMPTY, stat_ref[...])

        return carry

    lax.fori_loop(0, groups, step, 0)
    for n, ref in enumerate(o_refs):
        write_stat(ref, stat_ref[n * rows : (n + 1) * rows, :])


def weights_of(refs):
    stats = [read_stat(ref) for ref in refs]
    top = functools.reduce(jnp.maximum, stats)
    parts = [jnp.exp2(stat - top) for stat in stats]
    total = functools.reduce(jnp.add, parts)
    share = 1.0 / total
    return [part * share for part in parts], top + jnp.log2(total)


def combined(refs, weights, who):
    out = None
    for ref, weight in zip(refs, weights):
        part = ref[who].astype(F32) * weight[:, who : who + 1]
        out = part if out is None else out + part
    return out


def combine_kernel(*refs):
    *pieces, out_ref = refs
    weights, stat = weights_of(pieces)
    write_stat(out_ref, stat)
    for who in range(out_ref.shape[0] - 1):
        out_ref[who] = combined(pieces, weights, who).astype(BF16)


def project(latents, stats, proj_ref, out_ref):
    requests, steps, _ = out_ref.shape
    heads, _, width = proj_ref.shape
    latent = jnp.concatenate(latents, axis=0)
    stat = jnp.concatenate(stats, axis=0)
    shape = (latent.shape[0], width)
    head_of = lax.broadcasted_iota(jnp.int32, shape, 0) % heads

    def by_row(value):
        return value.reshape(requests * steps, heads, width).sum(axis=1)

    def put(value, at):
        for who in range(requests):
            out_ref[who, :, at : at + width] = value[who * steps : (who + 1) * steps]

    for h in range(heads):
        value = jnp.dot(latent, proj_ref[h], preferred_element_type=F32)
        put(by_row(jnp.where(head_of == h, value, 0.0)), h * width)
    lane = lax.broadcasted_iota(jnp.int32, shape, 1)
    put(by_row(jnp.where(head_of == lane, stat, 0.0)), heads * width)


def new_keys_kernel(q_ref, key_ref, proj_ref, out_ref):
    requests, rows, _ = q_ref.shape
    latent = proj_ref.shape[1]
    steps = key_ref.shape[1]
    heads = rows // steps
    step_of = lax.broadcasted_iota(jnp.int32, (rows, 1), 0) // heads
    latents, stats = [], []
    for who in range(requests):
        q = q_ref[who].astype(F32)
        keys = key_ref[who].astype(F32)
        scores = []
        for j in range(steps):
            s = jnp.sum(q * keys[j : j + 1, :], axis=1, keepdims=True) * score_scale
            scores.append(jnp.where(step_of >= j, s, -jnp.inf))
        top = functools.reduce(jnp.maximum, scores)
        parts = [jnp.exp2(s - top) for s in scores]
        total = functools.reduce(jnp.add, parts)
        out = None
        for j in range(steps):
            part = parts[j].astype(BF16).astype(F32) * keys[j : j + 1, :latent]
            out = part if out is None else out + part
        latents.append((out / total).astype(BF16))
        stats.append(top + jnp.log2(total))
    project(latents, stats, proj_ref, out_ref)


def finish_kernel(*refs):
    *pieces, proj_ref, out_ref = refs
    requests = out_ref.shape[0]
    weights, stat = weights_of(pieces)
    latents = [combined(pieces, weights, who).astype(BF16) for who in range(requests)]
    stats = [stat[:, who : who + 1] for who in range(requests)]
    project(latents, stats, proj_ref, out_ref)


def merge_kernel(cache_ref, new_ref, out_ref):
    width = out_ref.shape[2]
    heads = width // 128
    cache_stat = cache_ref[:, :, width:]
    new_stat = new_ref[:, :, width:]
    top = jnp.maximum(cache_stat, new_stat)
    cache_part = jnp.exp2(cache_stat - top)
    new_part = jnp.exp2(new_stat - top)
    share = 1.0 / (cache_part + new_part)
    cache_part = cache_part * share
    new_part = new_part * share
    for h in range(heads):
        at = slice(h * 128, (h + 1) * 128)
        value = cache_ref[:, :, at] * cache_part[:, :, h : h + 1]
        value = value + new_ref[:, :, at] * new_part[:, :, h : h + 1]
        out_ref[:, :, at] = value.astype(BF16)


def call(kernel, out_shape, *args, mib=12, **extra):
    return pl.pallas_call(
        kernel,
        out_shape=out_shape,
        compiler_params=pltpu.CompilerParams(vmem_limit_bytes=mib * MIB),
        **extra,
    )(*args)


def vmem(count):
    return [pl.BlockSpec(memory_space=pltpu.VMEM)] * count


def smem(count):
    return [pl.BlockSpec(memory_space=pltpu.SMEM)] * count


def combine(pieces):
    return call(
        combine_kernel,
        jax.ShapeDtypeStruct(pieces[0].shape, BF16),
        *pieces,
        in_specs=vmem(len(pieces)),
        out_specs=vmem(1)[0],
    )


def shards(block_pool, block_table, lengths, destination, query_latent, new_latent, value_proj):
    ring = lax.axis_size("seq")
    split_count = ring * lax.axis_size("dec")
    split_index = lax.axis_index(("seq", "dec"))
    requests = destination.shape[1]
    _, _, steps, heads, width = query_latent.shape
    rows = steps * heads
    latent, value_width = value_proj.shape[1:]
    block = block_pool.shape[4]
    slots = block_table.shape[3] // requests
    far, near = ring // 2, (ring - 1) // 2
    pool = jnp.swapaxes(block_pool[0, 0, 0], 1, 2)

    up = [(i, (i + 1) % ring) for i in range(ring)]
    down = [(i, (i - 1) % ring) for i in range(ring)]

    def swap(x):
        return lax.ppermute(x, "dec", [(0, 1), (1, 0)])

    decode_q = query_latent[0].reshape(requests, rows, width)
    own_q = lax.all_to_all(decode_q, "pre", split_axis=0, concat_axis=0, tiled=True)
    plan = call(
        functools.partial(plan_kernel, split_count, block),
        jax.ShapeDtypeStruct((requests, 3 + slots), jnp.int32),
        destination,
        lengths,
        block_table,
        split_index.reshape(1),
        in_specs=smem(4),
        out_specs=smem(1)[0],
        scratch_shapes=[pltpu.SMEM((slots // 2 + 1,), jnp.int32)],
    )
    values_shape = jax.ShapeDtypeStruct(
        (requests, steps, heads * value_width + 128), F32
    )
    new_values = call(
        new_keys_kernel,
        values_shape,
        decode_q,
        new_latent[0],
        value_proj,
        in_specs=vmem(3),
        out_specs=vmem(1)[0],
    )

    queries = {0: own_q}
    for s in range(1, far + 1):
        queries[-s] = lax.ppermute(queries[1 - s], "seq", up)
        if s <= near:
            queries[s] = lax.ppermute(queries[s - 1], "seq", down)
        if s == 1:
            queries[-s], plan = lax.optimization_barrier((queries[-s], plan))
        if s == 2:
            queries[-s], new_values = lax.optimization_barrier((queries[-s], new_values))
    order = sorted(queries)
    q_list = [queries[r] for r in order] + [swap(queries[r]) for r in order]
    n_pieces = len(q_list)
    piece = jax.ShapeDtypeStruct((requests + 1, rows, latent), BF16)
    outs = call(
        functools.partial(attention_kernel, n_pieces),
        [piece] * n_pieces,
        plan,
        *q_list,
        pool,
        in_specs=smem(1) + vmem(n_pieces) + [pl.BlockSpec(memory_space=pltpu.HBM)],
        out_specs=vmem(n_pieces),
        scratch_shapes=[
            pltpu.VMEM((2, GROUP, slots, width, block), BF16),
            pltpu.VMEM((n_pieces * rows, 128), F32),
            pltpu.SemaphoreType.DMA((2, GROUP, slots)),
        ],
        mib=50,
    )
    mine = dict(zip(order, outs[: len(order)]))
    others = {r: swap(x) for r, x in zip(order, outs[len(order) :])}

    from_up, from_down = [], []
    for s in range(far, 0, -1):
        sent = combine([mine[-s], others[-s]] + from_up)
        from_up = [lax.ppermute(sent, "seq", down)]
        if s <= near:
            sent = combine([mine[s], others[s]] + from_down)
            from_down = [lax.ppermute(sent, "seq", up)]
    pieces = [mine[0], others[0]] + from_up + from_down
    values = call(
        finish_kernel,
        values_shape,
        *pieces,
        value_proj,
        in_specs=vmem(len(pieces) + 1),
        out_specs=vmem(1)[0],
    )
    got = lax.all_to_all(values, "pre", split_axis=0, concat_axis=0, tiled=True)
    result = call(
        merge_kernel,
        jax.ShapeDtypeStruct((requests, steps, heads * value_width), BF16),
        got,
        new_values,
        in_specs=vmem(2),
        out_specs=vmem(1)[0],
    )
    return result[None]


def solution(mesh):
    return jax.shard_map(
        shards,
        mesh=mesh,
        in_specs=(
            P("pre", "seq", "dec", None, None, None),
            P("pre", "seq", "dec", None),
            P("pre", None),
            P("pre", None),
            P("pre", None, None, ("seq", "dec"), None),
            P("pre", None, None, None),
            P(("seq", "dec"), None, None),
        ),
        out_specs=P("pre", None, None, ("seq", "dec")),
        check_vma=False,
    )
```

```python
import functools

import jax
import jax.numpy as jnp
from jax import lax
from jax.experimental import pallas as pl
from jax.experimental.pallas import tpu as pltpu
from jax.sharding import PartitionSpec as P

score_scale = 192.0 ** (-0.5) * 1.4426950408889634
EMPTY = -(2.0**127)
F32 = jnp.float32
BF16 = jnp.bfloat16
MIB = 1024 * 1024
GROUP = 2


def pack_stat(stat):
    high = stat.astype(BF16)
    rest = stat - high.astype(F32)
    mid = rest.astype(BF16)
    low = (rest - mid.astype(F32)).astype(BF16)
    return high, mid, low


def read_stat(ref):
    requests = ref.shape[0] - 1
    parts = [ref[requests, :, i * 128 : (i + 1) * 128].astype(F32) for i in range(3)]
    return parts[0] + parts[1] + parts[2]


def write_stat(ref, stat):
    requests = ref.shape[0] - 1
    for i, part in enumerate(pack_stat(stat)):
        ref[requests, :, i * 128 : (i + 1) * 128] = part
    used = 3 * 128
    if ref.shape[2] > used:
        ref[requests, :, used:] = jnp.zeros((ref.shape[1], ref.shape[2] - used), BF16)


def plan_kernel(split_count, block, dest_ref, len_ref, table_ref, split_ref, out_ref, next_ref):
    requests = dest_ref.shape[1]
    slots = table_ref.shape[3] // requests
    split = split_ref[0]
    counts = []
    for i in range(requests):
        total = lax.div(len_ref[0, i] + (block - 1), block)
        counts.append(lax.div(total - split + (split_count - 1), split_count))
    pairs = [lax.div(count + 1, 2) for count in counts]
    for c in range(slots // 2 + 1):
        shorter = [(p < c).astype(jnp.int32) for p in pairs]
        next_ref[c] = functools.reduce(jnp.add, shorter)
    for i in range(requests):
        at = next_ref[pairs[i]]
        next_ref[pairs[i]] = at + 1
        start = (counts[i] - 1) * split_count + split
        used = (counts[i] - 1) * block + jnp.minimum(block, len_ref[0, i] - start * block)
        out_ref[at, 0] = dest_ref[0, i]
        out_ref[at, 1] = pairs[i]
        out_ref[at, 2] = jnp.where(counts[i] > 0, used, 0)
        for j in range(slots):
            out_ref[at, 3 + j] = table_ref[0, 0, 0, i * slots + j]


def attention_kernel(n_pieces, plan_ref, *refs):
    q_refs = refs[:n_pieces]
    pool_ref = refs[n_pieces]
    o_refs = refs[n_pieces + 1 : 2 * n_pieces + 1]
    kbuf, stat_ref, sems = refs[2 * n_pieces + 1 :]
    requests, rows, _ = q_refs[0].shape
    slots = plan_ref.shape[1] - 3
    block = pool_ref.shape[2]
    latent = o_refs[0].shape[2]
    groups = requests // GROUP

    def each(g, act):
        pairs = plan_ref[g * GROUP + GROUP - 1, 1]
        half = lax.rem(g, 2)
        for m in range(GROUP):
            for j in range(slots):

                @pl.when(j // 2 < pairs)
                def _():
                    act(
                        pltpu.make_async_copy(
                            pool_ref.at[plan_ref[g * GROUP + m, 3 + j]],
                            kbuf.at[half, m, j],
                            sems.at[half, m, j],
                        )
                    )

    each(0, lambda c: c.start())
    stat_ref[...] = jnp.zeros_like(stat_ref)
    lane = lax.broadcasted_iota(jnp.int32, stat_ref.shape, 1)
    pair = 2 * block
    column = lax.broadcasted_iota(jnp.int32, (1, pair), 1)

    def compute(g, pairs):
        half = lax.rem(g, 2)
        whos = [plan_ref[g * GROUP + m, 0] for m in range(GROUP)]
        keys, scores, tops = [], [], []
        for m, who in enumerate(whos):
            used = plan_ref[g * GROUP + m, 2]
            q = jnp.concatenate([ref[who] for ref in q_refs], axis=0)
            keys.append(
                [
                    jnp.concatenate([kbuf[half, m, 2 * c], kbuf[half, m, 2 * c + 1]], axis=1)
                    for c in range(pairs)
                ]
            )
            row = []
            for c in range(pairs):
                s = jnp.dot(q, keys[m][c], preferred_element_type=F32) * score_scale
                row.append(jnp.where(column < used - c * pair, s, -jnp.inf))
            scores.append(row)
        for row in scores:
            top = functools.reduce(jnp.maximum, row)
            tops.append(jnp.maximum(jnp.max(top, axis=1, keepdims=True), EMPTY))
        for m, who in enumerate(whos):
            total, out = None, None
            for c in range(pairs):
                e = jnp.exp2(scores[m][c] - tops[m])
                total = e if total is None else total + e
                part = lax.dot_general(
                    e.astype(BF16),
                    keys[m][c][:latent],
                    (((1,), (1,)), ((), ())),
                    preferred_element_type=F32,
                )
                out = part if out is None else out + part
            total = jnp.sum(total, axis=1, keepdims=True)
            some = total > 0
            out = (out * jnp.where(some, 1.0 / total, 0.0)).astype(BF16)
            for n, ref in enumerate(o_refs):
                ref[who] = out[n * rows : (n + 1) * rows]
            stat = jnp.where(some, tops[m] + jnp.log2(total), EMPTY)
            stat_ref[...] = jnp.where(lane == who, stat, stat_ref[...])

    def step(g, carry):
        @pl.when(g + 1 < groups)
        def _():
            each(g + 1, lambda c: c.start())

        each(g, lambda c: c.wait())
        pairs_here = plan_ref[g * GROUP + GROUP - 1, 1]
        for pairs in range(1, slots // 2 + 1):

            @pl.when(pairs_here == pairs)
            def _():
                compute(g, pairs)

        @pl.when(pairs_here == 0)
        def _():
            for m in range(GROUP):
                who = plan_ref[g * GROUP + m, 0]
                for ref in o_refs:
                    ref[who] = jnp.zeros((rows, latent), BF16)
                stat_ref[...] = jnp.where(lane == who, EMPTY, stat_ref[...])

        return carry

    lax.fori_loop(0, groups, step, 0)
    for n, ref in enumerate(o_refs):
        write_stat(ref, stat_ref[n * rows : (n + 1) * rows, :])


def weights_of(refs):
    stats = [read_stat(ref) for ref in refs]
    top = functools.reduce(jnp.maximum, stats)
    parts = [jnp.exp2(stat - top) for stat in stats]
    total = functools.reduce(jnp.add, parts)
    share = 1.0 / total
    return [part * share for part in parts], top + jnp.log2(total)


def combined(refs, weights, who):
    out = None
    for ref, weight in zip(refs, weights):
        part = ref[who].astype(F32) * weight[:, who : who + 1]
        out = part if out is None else out + part
    return out


def combine_kernel(*refs):
    *pieces, out_ref = refs
    weights, stat = weights_of(pieces)
    write_stat(out_ref, stat)
    for who in range(out_ref.shape[0] - 1):
        out_ref[who] = combined(pieces, weights, who).astype(BF16)


def project(latents, stats, proj_ref, out_ref):
    requests, steps, _ = out_ref.shape
    heads, _, width = proj_ref.shape
    latent = jnp.concatenate(latents, axis=0)
    stat = jnp.concatenate(stats, axis=0)
    shape = (latent.shape[0], width)
    head_of = lax.broadcasted_iota(jnp.int32, shape, 0) % heads

    def by_row(value):
        return value.reshape(requests * steps, heads, width).sum(axis=1)

    def put(value, at):
        for who in range(requests):
            out_ref[who, :, at : at + width] = value[who * steps : (who + 1) * steps]

    for h in range(heads):
        value = jnp.dot(latent, proj_ref[h], preferred_element_type=F32)
        put(by_row(jnp.where(head_of == h, value, 0.0)), h * width)
    lane = lax.broadcasted_iota(jnp.int32, shape, 1)
    put(by_row(jnp.where(head_of == lane, stat, 0.0)), heads * width)


def new_keys_kernel(q_ref, key_ref, proj_ref, out_ref):
    requests, rows, _ = q_ref.shape
    latent = proj_ref.shape[1]
    steps = key_ref.shape[1]
    heads = rows // steps
    step_of = lax.broadcasted_iota(jnp.int32, (rows, 1), 0) // heads
    latents, stats = [], []
    for who in range(requests):
        q = q_ref[who].astype(F32)
        keys = key_ref[who].astype(F32)
        scores = []
        for j in range(steps):
            s = jnp.sum(q * keys[j : j + 1, :], axis=1, keepdims=True) * score_scale
            scores.append(jnp.where(step_of >= j, s, -jnp.inf))
        top = functools.reduce(jnp.maximum, scores)
        parts = [jnp.exp2(s - top) for s in scores]
        total = functools.reduce(jnp.add, parts)
        out = None
        for j in range(steps):
            part = parts[j].astype(BF16).astype(F32) * keys[j : j + 1, :latent]
            out = part if out is None else out + part
        latents.append((out / total).astype(BF16))
        stats.append(top + jnp.log2(total))
    project(latents, stats, proj_ref, out_ref)


def finish_kernel(*refs):
    *pieces, proj_ref, out_ref = refs
    requests = out_ref.shape[0]
    weights, stat = weights_of(pieces)
    latents = [combined(pieces, weights, who).astype(BF16) for who in range(requests)]
    stats = [stat[:, who : who + 1] for who in range(requests)]
    project(latents, stats, proj_ref, out_ref)


def merge_kernel(cache_ref, new_ref, out_ref):
    width = out_ref.shape[2]
    heads = width // 128
    cache_stat = cache_ref[:, :, width:]
    new_stat = new_ref[:, :, width:]
    top = jnp.maximum(cache_stat, new_stat)
    cache_part = jnp.exp2(cache_stat - top)
    new_part = jnp.exp2(new_stat - top)
    share = 1.0 / (cache_part + new_part)
    cache_part = cache_part * share
    new_part = new_part * share
    for h in range(heads):
        at = slice(h * 128, (h + 1) * 128)
        value = cache_ref[:, :, at] * cache_part[:, :, h : h + 1]
        value = value + new_ref[:, :, at] * new_part[:, :, h : h + 1]
        out_ref[:, :, at] = value.astype(BF16)


def call(kernel, out_shape, *args, mib=12, **extra):
    return pl.pallas_call(
        kernel,
        out_shape=out_shape,
        compiler_params=pltpu.CompilerParams(vmem_limit_bytes=mib * MIB),
        **extra,
    )(*args)


def vmem(count):
    return [pl.BlockSpec(memory_space=pltpu.VMEM)] * count


def smem(count):
    return [pl.BlockSpec(memory_space=pltpu.SMEM)] * count


def combine(pieces):
    return call(
        combine_kernel,
        jax.ShapeDtypeStruct(pieces[0].shape, BF16),
        *pieces,
        in_specs=vmem(len(pieces)),
        out_specs=vmem(1)[0],
    )


def shards(block_pool, block_table, lengths, destination, query_latent, new_latent, value_proj):
    ring = lax.axis_size("seq")
    split_count = ring * lax.axis_size("dec")
    split_index = lax.axis_index(("seq", "dec"))
    requests = destination.shape[1]
    _, _, steps, heads, width = query_latent.shape
    rows = steps * heads
    latent, value_width = value_proj.shape[1:]
    block = block_pool.shape[4]
    slots = block_table.shape[3] // requests
    far, near = ring // 2, (ring - 1) // 2
    pool = jnp.swapaxes(block_pool[0, 0, 0], 1, 2)

    up = [(i, (i + 1) % ring) for i in range(ring)]
    down = [(i, (i - 1) % ring) for i in range(ring)]

    def swap(x):
        return lax.ppermute(x, "dec", [(0, 1), (1, 0)])

    decode_q = query_latent[0].reshape(requests, rows, width)
    own_q = lax.all_to_all(decode_q, "pre", split_axis=0, concat_axis=0, tiled=True)
    plan = call(
        functools.partial(plan_kernel, split_count, block),
        jax.ShapeDtypeStruct((requests, 3 + slots), jnp.int32),
        destination,
        lengths,
        block_table,
        split_index.reshape(1),
        in_specs=smem(4),
        out_specs=smem(1)[0],
        scratch_shapes=[pltpu.SMEM((slots // 2 + 1,), jnp.int32)],
    )
    values_shape = jax.ShapeDtypeStruct(
        (requests, steps, heads * value_width + 128), F32
    )
    new_values = call(
        new_keys_kernel,
        values_shape,
        decode_q,
        new_latent[0],
        value_proj,
        in_specs=vmem(3),
        out_specs=vmem(1)[0],
    )

    own_q, plan, new_values = lax.optimization_barrier((own_q, plan, new_values))

    queries = {0: own_q}
    for s in range(1, far + 1):
        queries[-s] = lax.ppermute(queries[1 - s], "seq", up)
        if s <= near:
            queries[s] = lax.ppermute(queries[s - 1], "seq", down)
    order = sorted(queries)
    q_list = [queries[r] for r in order] + [swap(queries[r]) for r in order]
    n_pieces = len(q_list)
    piece = jax.ShapeDtypeStruct((requests + 1, rows, latent), BF16)
    outs = call(
        functools.partial(attention_kernel, n_pieces),
        [piece] * n_pieces,
        plan,
        *q_list,
        pool,
        in_specs=smem(1) + vmem(n_pieces) + [pl.BlockSpec(memory_space=pltpu.HBM)],
        out_specs=vmem(n_pieces),
        scratch_shapes=[
            pltpu.VMEM((2, GROUP, slots, width, block), BF16),
            pltpu.VMEM((n_pieces * rows, 128), F32),
            pltpu.SemaphoreType.DMA((2, GROUP, slots)),
        ],
        mib=44,
    )
    mine = dict(zip(order, outs[: len(order)]))
    others = {r: swap(x) for r, x in zip(order, outs[len(order) :])}

    from_up, from_down = [], []
    for s in range(far, 0, -1):
        sent = combine([mine[-s], others[-s]] + from_up)
        from_up = [lax.ppermute(sent, "seq", down)]
        if s <= near:
            sent = combine([mine[s], others[s]] + from_down)
            from_down = [lax.ppermute(sent, "seq", up)]
    pieces = [mine[0], others[0]] + from_up + from_down
    values = call(
        finish_kernel,
        values_shape,
        *pieces,
        value_proj,
        in_specs=vmem(len(pieces) + 1),
        out_specs=vmem(1)[0],
    )
    got = lax.all_to_all(values, "pre", split_axis=0, concat_axis=0, tiled=True)
    result = call(
        merge_kernel,
        jax.ShapeDtypeStruct((requests, steps, heads * value_width), BF16),
        got,
        new_values,
        in_specs=vmem(2),
        out_specs=vmem(1)[0],
    )
    return result[None]


def solution(mesh):
    return jax.shard_map(
        shards,
        mesh=mesh,
        in_specs=(
            P("pre", "seq", "dec", None, None, None),
            P("pre", "seq", "dec", None),
            P("pre", None),
            P("pre", None),
            P("pre", None, None, ("seq", "dec"), None),
            P("pre", None, None, None),
            P(("seq", "dec"), None, None),
        ),
        out_specs=P("pre", None, None, ("seq", "dec")),
        check_vma=False,
    )
```

```python
import functools

import jax
import jax.numpy as jnp
from jax import lax
from jax.experimental import pallas as pl
from jax.experimental.pallas import tpu as pltpu
from jax.sharding import PartitionSpec as P

score_scale = 192.0 ** (-0.5) * 1.4426950408889634
EMPTY = -(2.0**127)
F32 = jnp.float32
BF16 = jnp.bfloat16
MIB = 1024 * 1024
GROUP = 2


def pack_stat(stat):
    high = stat.astype(BF16)
    rest = stat - high.astype(F32)
    mid = rest.astype(BF16)
    low = (rest - mid.astype(F32)).astype(BF16)
    return high, mid, low


def read_stat(ref):
    requests = ref.shape[0] - 1
    parts = [ref[requests, :, i * 128 : (i + 1) * 128].astype(F32) for i in range(3)]
    return parts[0] + parts[1] + parts[2]


def write_stat(ref, stat):
    requests = ref.shape[0] - 1
    for i, part in enumerate(pack_stat(stat)):
        ref[requests, :, i * 128 : (i + 1) * 128] = part
    used = 3 * 128
    if ref.shape[2] > used:
        ref[requests, :, used:] = jnp.zeros((ref.shape[1], ref.shape[2] - used), BF16)


def plan_kernel(split_count, block, dest_ref, len_ref, table_ref, split_ref, out_ref, next_ref):
    requests = dest_ref.shape[1]
    slots = table_ref.shape[3] // requests
    split = split_ref[0]
    counts = []
    for i in range(requests):
        total = lax.div(len_ref[0, i] + (block - 1), block)
        counts.append(lax.div(total - split + (split_count - 1), split_count))
    pairs = [lax.div(count + 1, 2) for count in counts]
    for c in range(slots // 2 + 1):
        shorter = [(p < c).astype(jnp.int32) for p in pairs]
        next_ref[c] = functools.reduce(jnp.add, shorter)
    for i in range(requests):
        at = next_ref[pairs[i]]
        next_ref[pairs[i]] = at + 1
        start = (counts[i] - 1) * split_count + split
        used = (counts[i] - 1) * block + jnp.minimum(block, len_ref[0, i] - start * block)
        out_ref[at, 0] = dest_ref[0, i]
        out_ref[at, 1] = pairs[i]
        out_ref[at, 2] = jnp.where(counts[i] > 0, used, 0)
        for j in range(slots):
            out_ref[at, 3 + j] = table_ref[0, 0, 0, i * slots + j]


def as_pieces(refs):
    per_core = len(refs) // 2
    pieces = []
    for core in (refs[:per_core], refs[per_core:]):
        pieces += [core[:2]] + [(ref,) for ref in core[2:]]
    return pieces


def load(piece, who):
    if len(piece) == 1:
        return piece[0][who]
    first, second = piece
    half = first.shape[0]
    low = first[jnp.minimum(who, half - 1)]
    high = second[jnp.maximum(who - half, 0)]
    return jnp.where(who < half, low, high)


def store(piece, who, value):
    if len(piece) == 1:
        piece[0][who] = value
        return
    first, second = piece
    half = first.shape[0] - 1

    @pl.when(who < half)
    def _():
        first[who] = value

    @pl.when(who >= half)
    def _():
        second[who - half] = value


def attention_kernel(n_pieces, plan_ref, *refs):
    n_refs = n_pieces + 2
    q_pieces = as_pieces(refs[:n_refs])
    pool_ref = refs[n_refs]
    o_pieces = as_pieces(refs[n_refs + 1 : 2 * n_refs + 1])
    kbuf, stat_ref, sems = refs[2 * n_refs + 1 :]
    requests, rows, _ = q_pieces[1][0].shape
    slots = plan_ref.shape[1] - 3
    block = pool_ref.shape[2]
    latent = o_pieces[0][0].shape[2]
    groups = requests // GROUP

    def each(g, act):
        pairs = plan_ref[g * GROUP + GROUP - 1, 1]
        half = lax.rem(g, 2)
        for m in range(GROUP):
            for j in range(slots):

                @pl.when(j // 2 < pairs)
                def _():
                    act(
                        pltpu.make_async_copy(
                            pool_ref.at[plan_ref[g * GROUP + m, 3 + j]],
                            kbuf.at[half, m, j],
                            sems.at[half, m, j],
                        )
                    )

    each(0, lambda c: c.start())
    stat_ref[...] = jnp.zeros_like(stat_ref)
    lane = lax.broadcasted_iota(jnp.int32, stat_ref.shape, 1)
    pair = 2 * block
    column = lax.broadcasted_iota(jnp.int32, (1, pair), 1)

    def compute(g, pairs):
        half = lax.rem(g, 2)
        whos = [plan_ref[g * GROUP + m, 0] for m in range(GROUP)]
        keys, scores, tops = [], [], []
        for m, who in enumerate(whos):
            used = plan_ref[g * GROUP + m, 2]
            q = jnp.concatenate([load(piece, who) for piece in q_pieces], axis=0)
            keys.append(
                [
                    jnp.concatenate([kbuf[half, m, 2 * c], kbuf[half, m, 2 * c + 1]], axis=1)
                    for c in range(pairs)
                ]
            )
            row = []
            for c in range(pairs):
                s = jnp.dot(q, keys[m][c], preferred_element_type=F32) * score_scale
                row.append(jnp.where(column < used - c * pair, s, -jnp.inf))
            scores.append(row)
        for row in scores:
            top = functools.reduce(jnp.maximum, row)
            tops.append(jnp.maximum(jnp.max(top, axis=1, keepdims=True), EMPTY))
        for m, who in enumerate(whos):
            total, out = None, None
            for c in range(pairs):
                e = jnp.exp2(scores[m][c] - tops[m])
                total = e if total is None else total + e
                part = lax.dot_general(
                    e.astype(BF16),
                    keys[m][c][:latent],
                    (((1,), (1,)), ((), ())),
                    preferred_element_type=F32,
                )
                out = part if out is None else out + part
            total = jnp.sum(total, axis=1, keepdims=True)
            some = total > 0
            out = (out * jnp.where(some, 1.0 / total, 0.0)).astype(BF16)
            for n, piece in enumerate(o_pieces):
                store(piece, who, out[n * rows : (n + 1) * rows])
            stat = jnp.where(some, tops[m] + jnp.log2(total), EMPTY)
            stat_ref[...] = jnp.where(lane == who, stat, stat_ref[...])

    def step(g, carry):
        @pl.when(g + 1 < groups)
        def _():
            each(g + 1, lambda c: c.start())

        each(g, lambda c: c.wait())
        pairs_here = plan_ref[g * GROUP + GROUP - 1, 1]
        for pairs in range(1, slots // 2 + 1):

            @pl.when(pairs_here == pairs)
            def _():
                compute(g, pairs)

        @pl.when(pairs_here == 0)
        def _():
            for m in range(GROUP):
                who = plan_ref[g * GROUP + m, 0]
                for piece in o_pieces:
                    store(piece, who, jnp.zeros((rows, latent), BF16))
                stat_ref[...] = jnp.where(lane == who, EMPTY, stat_ref[...])

        return carry

    lax.fori_loop(0, groups, step, 0)
    for n, piece in enumerate(o_pieces):
        for ref in piece:
            write_stat(ref, stat_ref[n * rows : (n + 1) * rows, :])


def weights_of(refs, spans):
    stats = []
    for ref, (first, last) in zip(refs, spans):
        stat = read_stat(ref)
        lane = lax.broadcasted_iota(jnp.int32, stat.shape, 1)
        stats.append(jnp.where((lane >= first) & (lane < last), stat, EMPTY))
    top = functools.reduce(jnp.maximum, stats)
    parts = [jnp.exp2(stat - top) for stat in stats]
    total = functools.reduce(jnp.add, parts)
    share = 1.0 / total
    return [part * share for part in parts], top + jnp.log2(total)


def combined(refs, spans, weights, who):
    out = None
    for ref, (first, last), weight in zip(refs, spans, weights):
        if first <= who < last:
            part = ref[who - first].astype(F32) * weight[:, who : who + 1]
            out = part if out is None else out + part
    return out


def combine_kernel(spans, *refs):
    *pieces, out_ref = refs
    weights, stat = weights_of(pieces, spans)
    write_stat(out_ref, stat)
    first, last = spans[0]
    for who in range(first, last):
        out_ref[who - first] = combined(pieces, spans, weights, who).astype(BF16)


def project(latents, stats, proj_ref, out_ref):
    requests, steps, _ = out_ref.shape
    heads, _, width = proj_ref.shape
    latent = jnp.concatenate(latents, axis=0)
    stat = jnp.concatenate(stats, axis=0)
    shape = (latent.shape[0], width)
    head_of = lax.broadcasted_iota(jnp.int32, shape, 0) % heads

    def by_row(value):
        return value.reshape(requests * steps, heads, width).sum(axis=1)

    def put(value, at):
        for who in range(requests):
            out_ref[who, :, at : at + width] = value[who * steps : (who + 1) * steps]

    for h in range(heads):
        value = jnp.dot(latent, proj_ref[h], preferred_element_type=F32)
        put(by_row(jnp.where(head_of == h, value, 0.0)), h * width)
    lane = lax.broadcasted_iota(jnp.int32, shape, 1)
    put(by_row(jnp.where(head_of == lane, stat, 0.0)), heads * width)


def new_keys_kernel(q_ref, key_ref, proj_ref, out_ref):
    requests, rows, _ = q_ref.shape
    latent = proj_ref.shape[1]
    steps = key_ref.shape[1]
    heads = rows // steps
    step_of = lax.broadcasted_iota(jnp.int32, (rows, 1), 0) // heads
    latents, stats = [], []
    for who in range(requests):
        q = q_ref[who].astype(F32)
        keys = key_ref[who].astype(F32)
        scores = []
        for j in range(steps):
            s = jnp.sum(q * keys[j : j + 1, :], axis=1, keepdims=True) * score_scale
            scores.append(jnp.where(step_of >= j, s, -jnp.inf))
        top = functools.reduce(jnp.maximum, scores)
        parts = [jnp.exp2(s - top) for s in scores]
        total = functools.reduce(jnp.add, parts)
        out = None
        for j in range(steps):
            part = parts[j].astype(BF16).astype(F32) * keys[j : j + 1, :latent]
            out = part if out is None else out + part
        latents.append((out / total).astype(BF16))
        stats.append(top + jnp.log2(total))
    project(latents, stats, proj_ref, out_ref)


def finish_kernel(*refs):
    *pieces, proj_ref, out_ref = refs
    requests = out_ref.shape[0]
    spans = [(0, requests)] * len(pieces)
    weights, stat = weights_of(pieces, spans)
    latents = [
        combined(pieces, spans, weights, who).astype(BF16) for who in range(requests)
    ]
    stats = [stat[:, who : who + 1] for who in range(requests)]
    project(latents, stats, proj_ref, out_ref)


def merge_kernel(cache_ref, new_ref, out_ref):
    width = out_ref.shape[2]
    heads = width // 128
    cache_stat = cache_ref[:, :, width:]
    new_stat = new_ref[:, :, width:]
    top = jnp.maximum(cache_stat, new_stat)
    cache_part = jnp.exp2(cache_stat - top)
    new_part = jnp.exp2(new_stat - top)
    share = 1.0 / (cache_part + new_part)
    cache_part = cache_part * share
    new_part = new_part * share
    for h in range(heads):
        at = slice(h * 128, (h + 1) * 128)
        value = cache_ref[:, :, at] * cache_part[:, :, h : h + 1]
        value = value + new_ref[:, :, at] * new_part[:, :, h : h + 1]
        out_ref[:, :, at] = value.astype(BF16)


def call(kernel, out_shape, *args, mib=12, **extra):
    return pl.pallas_call(
        kernel,
        out_shape=out_shape,
        compiler_params=pltpu.CompilerParams(vmem_limit_bytes=mib * MIB),
        **extra,
    )(*args)


def vmem(count):
    return [pl.BlockSpec(memory_space=pltpu.VMEM)] * count


def smem(count):
    return [pl.BlockSpec(memory_space=pltpu.SMEM)] * count


def combine(pieces):
    arrays = [array for array, _ in pieces]
    spans = tuple(span for _, span in pieces)
    out = call(
        functools.partial(combine_kernel, spans),
        jax.ShapeDtypeStruct(arrays[0].shape, BF16),
        *arrays,
        in_specs=vmem(len(pieces)),
        out_specs=vmem(1)[0],
    )
    return out, spans[0]


def shards(block_pool, block_table, lengths, destination, query_latent, new_latent, value_proj):
    ring = lax.axis_size("seq")
    split_count = ring * lax.axis_size("dec")
    split_index = lax.axis_index(("seq", "dec"))
    requests = destination.shape[1]
    _, _, steps, heads, width = query_latent.shape
    rows = steps * heads
    latent, value_width = value_proj.shape[1:]
    block = block_pool.shape[4]
    slots = block_table.shape[3] // requests
    far = ring // 2
    pool = jnp.swapaxes(block_pool[0, 0, 0], 1, 2)

    up = [(i, (i + 1) % ring) for i in range(ring)]
    down = [(i, (i - 1) % ring) for i in range(ring)]

    def swap(x):
        return lax.ppermute(x, "dec", [(0, 1), (1, 0)])

    decode_q = query_latent[0].reshape(requests, rows, width)
    own_q = lax.all_to_all(decode_q, "pre", split_axis=0, concat_axis=0, tiled=True)
    plan = call(
        functools.partial(plan_kernel, split_count, block),
        jax.ShapeDtypeStruct((requests, 3 + slots), jnp.int32),
        destination,
        lengths,
        block_table,
        split_index.reshape(1),
        in_specs=smem(4),
        out_specs=smem(1)[0],
        scratch_shapes=[pltpu.SMEM((slots // 2 + 1,), jnp.int32)],
    )
    values_shape = jax.ShapeDtypeStruct(
        (requests, steps, heads * value_width + 128), F32
    )
    new_values = call(
        new_keys_kernel,
        values_shape,
        decode_q,
        new_latent[0],
        value_proj,
        in_specs=vmem(3),
        out_specs=vmem(1)[0],
    )

    own_q, plan, new_values = lax.optimization_barrier((own_q, plan, new_values))

    half = requests // 2
    queries = {0: own_q}
    for s in range(1, far):
        queries[-s] = lax.ppermute(queries[1 - s], "seq", up)
        queries[s] = lax.ppermute(queries[s - 1], "seq", down)
    halves = [
        lax.ppermute(queries[1 - far][:half], "seq", up),
        lax.ppermute(queries[far - 1][half:], "seq", down),
    ]
    order = sorted(queries)
    early = [r for r in order if abs(r) < far - 2]
    late = [r for r in order if abs(r) >= far - 2]
    waited = early + [2 - far, far - 2]
    tied = dict(zip(waited, lax.optimization_barrier([queries[r] for r in waited])))
    tied.update(zip(late, lax.optimization_barrier([queries[r] for r in late])))
    near_by = [tied[r] for r in order]
    q_list = halves + near_by + [swap(x) for x in near_by + halves]
    q_list = q_list[: len(order) + 2] + q_list[-2:] + q_list[len(order) + 2 : -2]
    n_pieces = 2 * (len(order) + 1)
    half_piece = jax.ShapeDtypeStruct((half + 1, rows, latent), BF16)
    piece = jax.ShapeDtypeStruct((requests + 1, rows, latent), BF16)
    shapes = ([half_piece] * 2 + [piece] * len(order)) * 2
    outs = call(
        functools.partial(attention_kernel, n_pieces),
        shapes,
        plan,
        *q_list,
        pool,
        in_specs=smem(1) + vmem(len(q_list)) + [pl.BlockSpec(memory_space=pltpu.HBM)],
        out_specs=vmem(len(q_list)),
        scratch_shapes=[
            pltpu.VMEM((2, GROUP, slots, width, block), BF16),
            pltpu.VMEM((n_pieces * rows, 128), F32),
            pltpu.SemaphoreType.DMA((2, GROUP, slots)),
        ],
        mib=44,
    )
    per_core = len(outs) // 2
    everything, low, high = (0, requests), (0, half), (half, requests)
    names = ["low", "high"] + order
    span_of = {"low": low, "high": high}
    both = {}
    for name, own, other in zip(names, outs[:per_core], outs[per_core:]):
        span = span_of.get(name, everything)
        both[name] = [(own, span), (swap(other), span)]

    def passed(name, arrived, way):
        sent, span = combine(both[name] + arrived)
        return [(lax.ppermute(sent, "seq", way), span)]

    from_up = passed("low", [], down)
    from_down = passed("high", [], up)
    for s in range(far - 1, 0, -1):
        from_up = passed(-s, from_up, down)
        from_down = passed(s, from_down, up)
    pieces = [array for array, _ in both[0] + from_up + from_down]
    values = call(
        finish_kernel,
        values_shape,
        *pieces,
        value_proj,
        in_specs=vmem(len(pieces) + 1),
        out_specs=vmem(1)[0],
    )
    got = lax.all_to_all(values, "pre", split_axis=0, concat_axis=0, tiled=True)
    result = call(
        merge_kernel,
        jax.ShapeDtypeStruct((requests, steps, heads * value_width), BF16),
        got,
        new_values,
        in_specs=vmem(2),
        out_specs=vmem(1)[0],
    )
    return result[None]


def solution(mesh):
    return jax.shard_map(
        shards,
        mesh=mesh,
        in_specs=(
            P("pre", "seq", "dec", None, None, None),
            P("pre", "seq", "dec", None),
            P("pre", None),
            P("pre", None),
            P("pre", None, None, ("seq", "dec"), None),
            P("pre", None, None, None),
            P(("seq", "dec"), None, None),
        ),
        out_specs=P("pre", None, None, ("seq", "dec")),
        check_vma=False,
    )
```

```python
import functools

import jax
import jax.numpy as jnp
from jax import lax
from jax.experimental import pallas as pl
from jax.experimental.pallas import tpu as pltpu
from jax.sharding import PartitionSpec as P

score_scale = 192.0 ** (-0.5) * 1.4426950408889634
EMPTY = -(2.0**127)
F32 = jnp.float32
BF16 = jnp.bfloat16
MIB = 1024 * 1024
GROUP = 2


def pack_stat(stat):
    high = stat.astype(BF16)
    rest = stat - high.astype(F32)
    mid = rest.astype(BF16)
    low = (rest - mid.astype(F32)).astype(BF16)
    return high, mid, low


def read_stat(ref):
    requests = ref.shape[0] - 1
    parts = [ref[requests, :, i * 128 : (i + 1) * 128].astype(F32) for i in range(3)]
    return parts[0] + parts[1] + parts[2]


def write_stat(ref, stat):
    requests = ref.shape[0] - 1
    for i, part in enumerate(pack_stat(stat)):
        ref[requests, :, i * 128 : (i + 1) * 128] = part
    used = 3 * 128
    if ref.shape[2] > used:
        ref[requests, :, used:] = jnp.zeros((ref.shape[1], ref.shape[2] - used), BF16)


def plan_kernel(split_count, block, dest_ref, len_ref, table_ref, split_ref, out_ref, next_ref):
    requests = dest_ref.shape[1]
    slots = table_ref.shape[3] // requests
    split = split_ref[0]
    counts = []
    for i in range(requests):
        total = lax.div(len_ref[0, i] + (block - 1), block)
        counts.append(lax.div(total - split + (split_count - 1), split_count))
    pairs = [lax.div(count + 1, 2) for count in counts]
    for c in range(slots // 2 + 1):
        shorter = [(p < c).astype(jnp.int32) for p in pairs]
        next_ref[c] = functools.reduce(jnp.add, shorter)
    for i in range(requests):
        at = next_ref[pairs[i]]
        next_ref[pairs[i]] = at + 1
        start = (counts[i] - 1) * split_count + split
        used = (counts[i] - 1) * block + jnp.minimum(block, len_ref[0, i] - start * block)
        out_ref[at, 0] = dest_ref[0, i]
        out_ref[at, 1] = pairs[i]
        out_ref[at, 2] = jnp.where(counts[i] > 0, used, 0)
        for j in range(slots):
            out_ref[at, 3 + j] = table_ref[0, 0, 0, i * slots + j]


def attention_kernel(n_pieces, plan_ref, *refs):
    q_refs = refs[:n_pieces]
    pool_ref = refs[n_pieces]
    o_refs = refs[n_pieces + 1 : 2 * n_pieces + 1]
    kbuf, stat_ref, sems = refs[2 * n_pieces + 1 :]
    requests, rows, _ = q_refs[0].shape
    slots = plan_ref.shape[1] - 3
    block = pool_ref.shape[2]
    latent = o_refs[0].shape[2]
    groups = requests // GROUP

    def each(g, act):
        pairs = plan_ref[g * GROUP + GROUP - 1, 1]
        half = lax.rem(g, 2)
        for m in range(GROUP):
            for j in range(slots):

                @pl.when(j // 2 < pairs)
                def _():
                    act(
                        pltpu.make_async_copy(
                            pool_ref.at[plan_ref[g * GROUP + m, 3 + j]],
                            kbuf.at[half, m, j],
                            sems.at[half, m, j],
                        )
                    )

    each(0, lambda c: c.start())
    stat_ref[...] = jnp.zeros_like(stat_ref)
    lane = lax.broadcasted_iota(jnp.int32, stat_ref.shape, 1)
    pair = 2 * block
    column = lax.broadcasted_iota(jnp.int32, (1, pair), 1)

    def compute(g, pairs):
        half = lax.rem(g, 2)
        whos = [plan_ref[g * GROUP + m, 0] for m in range(GROUP)]
        keys, scores, tops = [], [], []
        for m, who in enumerate(whos):
            used = plan_ref[g * GROUP + m, 2]
            q = jnp.concatenate([ref[who] for ref in q_refs], axis=0)
            keys.append(
                [
                    jnp.concatenate([kbuf[half, m, 2 * c], kbuf[half, m, 2 * c + 1]], axis=1)
                    for c in range(pairs)
                ]
            )
            row = []
            for c in range(pairs):
                s = jnp.dot(q, keys[m][c], preferred_element_type=F32) * score_scale
                row.append(jnp.where(column < used - c * pair, s, -jnp.inf))
            scores.append(row)
        for row in scores:
            top = functools.reduce(jnp.maximum, row)
            tops.append(jnp.maximum(jnp.max(top, axis=1, keepdims=True), EMPTY))
        for m, who in enumerate(whos):
            total, out = None, None
            for c in range(pairs):
                e = jnp.exp2(scores[m][c] - tops[m])
                total = e if total is None else total + e
                part = lax.dot_general(
                    e.astype(BF16),
                    keys[m][c][:latent],
                    (((1,), (1,)), ((), ())),
                    preferred_element_type=F32,
                )
                out = part if out is None else out + part
            total = jnp.sum(total, axis=1, keepdims=True)
            some = total > 0
            out = (out * jnp.where(some, 1.0 / total, 0.0)).astype(BF16)
            for n, ref in enumerate(o_refs):
                ref[who] = out[n * rows : (n + 1) * rows]
            stat = jnp.where(some, tops[m] + jnp.log2(total), EMPTY)
            stat_ref[...] = jnp.where(lane == who, stat, stat_ref[...])

    def step(g, carry):
        @pl.when(g + 1 < groups)
        def _():
            each(g + 1, lambda c: c.start())

        each(g, lambda c: c.wait())
        pairs_here = plan_ref[g * GROUP + GROUP - 1, 1]
        for pairs in range(1, slots // 2 + 1):

            @pl.when(pairs_here == pairs)
            def _():
                compute(g, pairs)

        @pl.when(pairs_here == 0)
        def _():
            for m in range(GROUP):
                who = plan_ref[g * GROUP + m, 0]
                for ref in o_refs:
                    ref[who] = jnp.zeros((rows, latent), BF16)
                stat_ref[...] = jnp.where(lane == who, EMPTY, stat_ref[...])

        return carry

    lax.fori_loop(0, groups, step, 0)
    for n, ref in enumerate(o_refs):
        write_stat(ref, stat_ref[n * rows : (n + 1) * rows, :])


def weights_of(refs, spans):
    stats = []
    for ref, (first, last) in zip(refs, spans):
        stat = read_stat(ref)
        lane = lax.broadcasted_iota(jnp.int32, stat.shape, 1)
        stats.append(jnp.where((lane >= first) & (lane < last), stat, EMPTY))
    top = functools.reduce(jnp.maximum, stats)
    parts = [jnp.exp2(stat - top) for stat in stats]
    total = functools.reduce(jnp.add, parts)
    share = 1.0 / total
    return [part * share for part in parts], top + jnp.log2(total)


def combined(refs, spans, weights, who):
    out = None
    for ref, (first, last), weight in zip(refs, spans, weights):
        if first <= who < last:
            part = ref[who - first].astype(F32) * weight[:, who : who + 1]
            out = part if out is None else out + part
    return out


def combine_kernel(spans, out_spans, *refs):
    pieces, out_refs = refs[: len(spans)], refs[len(spans) :]
    weights, stat = weights_of(pieces, spans)
    for out_ref, (first, last) in zip(out_refs, out_spans):
        write_stat(out_ref, stat)
        for who in range(first, last):
            out_ref[who - first] = combined(pieces, spans, weights, who).astype(BF16)


def project(latents, stats, proj_ref, out_ref):
    requests, steps, _ = out_ref.shape
    heads, _, width = proj_ref.shape
    latent = jnp.concatenate(latents, axis=0)
    stat = jnp.concatenate(stats, axis=0)
    shape = (latent.shape[0], width)
    head_of = lax.broadcasted_iota(jnp.int32, shape, 0) % heads

    def by_row(value):
        return value.reshape(requests * steps, heads, width).sum(axis=1)

    def put(value, at):
        for who in range(requests):
            out_ref[who, :, at : at + width] = value[who * steps : (who + 1) * steps]

    for h in range(heads):
        value = jnp.dot(latent, proj_ref[h], preferred_element_type=F32)
        put(by_row(jnp.where(head_of == h, value, 0.0)), h * width)
    lane = lax.broadcasted_iota(jnp.int32, shape, 1)
    put(by_row(jnp.where(head_of == lane, stat, 0.0)), heads * width)


def new_keys_kernel(q_ref, key_ref, proj_ref, out_ref):
    requests, rows, _ = q_ref.shape
    latent = proj_ref.shape[1]
    steps = key_ref.shape[1]
    heads = rows // steps
    step_of = lax.broadcasted_iota(jnp.int32, (rows, 1), 0) // heads
    latents, stats = [], []
    for who in range(requests):
        q = q_ref[who].astype(F32)
        keys = key_ref[who].astype(F32)
        scores = []
        for j in range(steps):
            s = jnp.sum(q * keys[j : j + 1, :], axis=1, keepdims=True) * score_scale
            scores.append(jnp.where(step_of >= j, s, -jnp.inf))
        top = functools.reduce(jnp.maximum, scores)
        parts = [jnp.exp2(s - top) for s in scores]
        total = functools.reduce(jnp.add, parts)
        out = None
        for j in range(steps):
            part = parts[j].astype(BF16).astype(F32) * keys[j : j + 1, :latent]
            out = part if out is None else out + part
        latents.append((out / total).astype(BF16))
        stats.append(top + jnp.log2(total))
    project(latents, stats, proj_ref, out_ref)


def finish_kernel(*refs):
    *pieces, proj_ref, out_ref = refs
    requests = out_ref.shape[0]
    spans = [(0, requests)] * len(pieces)
    weights, stat = weights_of(pieces, spans)
    latents = [
        combined(pieces, spans, weights, who).astype(BF16) for who in range(requests)
    ]
    stats = [stat[:, who : who + 1] for who in range(requests)]
    project(latents, stats, proj_ref, out_ref)


def merge_kernel(cache_ref, new_ref, out_ref):
    width = out_ref.shape[2]
    heads = width // 128
    cache_stat = cache_ref[:, :, width:]
    new_stat = new_ref[:, :, width:]
    top = jnp.maximum(cache_stat, new_stat)
    cache_part = jnp.exp2(cache_stat - top)
    new_part = jnp.exp2(new_stat - top)
    share = 1.0 / (cache_part + new_part)
    cache_part = cache_part * share
    new_part = new_part * share
    for h in range(heads):
        at = slice(h * 128, (h + 1) * 128)
        value = cache_ref[:, :, at] * cache_part[:, :, h : h + 1]
        value = value + new_ref[:, :, at] * new_part[:, :, h : h + 1]
        out_ref[:, :, at] = value.astype(BF16)


def call(kernel, out_shape, *args, mib=12, **extra):
    return pl.pallas_call(
        kernel,
        out_shape=out_shape,
        compiler_params=pltpu.CompilerParams(vmem_limit_bytes=mib * MIB),
        **extra,
    )(*args)


def vmem(count):
    return [pl.BlockSpec(memory_space=pltpu.VMEM)] * count


def smem(count):
    return [pl.BlockSpec(memory_space=pltpu.SMEM)] * count


def combine(pieces, out_spans):
    arrays = [array for array, _ in pieces]
    spans = tuple(span for _, span in pieces)
    shapes = [
        jax.ShapeDtypeStruct((last - first + 1,) + arrays[0].shape[1:], BF16)
        for first, last in out_spans
    ]
    outs = call(
        functools.partial(combine_kernel, spans, tuple(out_spans)),
        shapes,
        *arrays,
        in_specs=vmem(len(arrays)),
        out_specs=vmem(len(shapes)),
    )
    return list(zip(outs, out_spans))


def shards(block_pool, block_table, lengths, destination, query_latent, new_latent, value_proj):
    ring = lax.axis_size("seq")
    split_count = ring * lax.axis_size("dec")
    split_index = lax.axis_index(("seq", "dec"))
    requests = destination.shape[1]
    _, _, steps, heads, width = query_latent.shape
    rows = steps * heads
    latent, value_width = value_proj.shape[1:]
    block = block_pool.shape[4]
    slots = block_table.shape[3] // requests
    far, near = ring // 2, (ring - 1) // 2
    pool = jnp.swapaxes(block_pool[0, 0, 0], 1, 2)

    up = [(i, (i + 1) % ring) for i in range(ring)]
    down = [(i, (i - 1) % ring) for i in range(ring)]

    def swap(x):
        return lax.ppermute(x, "dec", [(0, 1), (1, 0)])

    decode_q = query_latent[0].reshape(requests, rows, width)
    own_q = lax.all_to_all(decode_q, "pre", split_axis=0, concat_axis=0, tiled=True)
    plan = call(
        functools.partial(plan_kernel, split_count, block),
        jax.ShapeDtypeStruct((requests, 3 + slots), jnp.int32),
        destination,
        lengths,
        block_table,
        split_index.reshape(1),
        in_specs=smem(4),
        out_specs=smem(1)[0],
        scratch_shapes=[pltpu.SMEM((slots // 2 + 1,), jnp.int32)],
    )
    values_shape = jax.ShapeDtypeStruct(
        (requests, steps, heads * value_width + 128), F32
    )
    new_values = call(
        new_keys_kernel,
        values_shape,
        decode_q,
        new_latent[0],
        value_proj,
        in_specs=vmem(3),
        out_specs=vmem(1)[0],
    )

    queries = {0: own_q}
    for s in range(1, far + 1):
        queries[-s] = lax.ppermute(queries[1 - s], "seq", up)
        if s <= near:
            queries[s] = lax.ppermute(queries[s - 1], "seq", down)
        if s == 1:
            queries[-s], plan = lax.optimization_barrier((queries[-s], plan))
        if s == 2:
            queries[-s], new_values = lax.optimization_barrier((queries[-s], new_values))
    order = sorted(queries)
    q_list = [queries[r] for r in order] + [swap(queries[r]) for r in order]
    n_pieces = len(q_list)
    piece = jax.ShapeDtypeStruct((requests + 1, rows, latent), BF16)
    outs = call(
        functools.partial(attention_kernel, n_pieces),
        [piece] * n_pieces,
        plan,
        *q_list,
        pool,
        in_specs=smem(1) + vmem(n_pieces) + [pl.BlockSpec(memory_space=pltpu.HBM)],
        out_specs=vmem(n_pieces),
        scratch_shapes=[
            pltpu.VMEM((2, GROUP, slots, width, block), BF16),
            pltpu.VMEM((n_pieces * rows, 128), F32),
            pltpu.SemaphoreType.DMA((2, GROUP, slots)),
        ],
        mib=44,
    )
    everything = (0, requests)
    both = {
        r: [(own, everything), (swap(other), everything)]
        for r, own, other in zip(order, outs[: len(order)], outs[len(order) :])
    }

    def sent(piece, way):
        array, span = piece
        return [(lax.ppermute(array, "seq", way), span)]

    halves = [(0, requests // 2), (requests // 2, requests)]
    low, high = combine(both[-far], halves)
    from_up, from_down = sent(low, down), sent(high, up)
    for s in range(far - 1, 0, -1):
        from_up = sent(combine(both[-s] + from_up, [everything])[0], down)
        from_down = sent(combine(both[s] + from_down, [everything])[0], up)
    pieces = [array for array, _ in both[0] + from_up + from_down]
    values = call(
        finish_kernel,
        values_shape,
        *pieces,
        value_proj,
        in_specs=vmem(len(pieces) + 1),
        out_specs=vmem(1)[0],
    )
    got = lax.all_to_all(values, "pre", split_axis=0, concat_axis=0, tiled=True)
    result = call(
        merge_kernel,
        jax.ShapeDtypeStruct((requests, steps, heads * value_width), BF16),
        got,
        new_values,
        in_specs=vmem(2),
        out_specs=vmem(1)[0],
    )
    return result[None]


def solution(mesh):
    return jax.shard_map(
        shards,
        mesh=mesh,
        in_specs=(
            P("pre", "seq", "dec", None, None, None),
            P("pre", "seq", "dec", None),
            P("pre", None),
            P("pre", None),
            P("pre", None, None, ("seq", "dec"), None),
            P("pre", None, None, None),
            P(("seq", "dec"), None, None),
        ),
        out_specs=P("pre", None, None, ("seq", "dec")),
        check_vma=False,
    )
```

```python
import functools

import jax
import jax.numpy as jnp
from jax import lax
from jax.experimental import pallas as pl
from jax.experimental.pallas import tpu as pltpu
from jax.sharding import PartitionSpec as P

score_scale = 192.0 ** (-0.5) * 1.4426950408889634
EMPTY = -(2.0**127)
F32 = jnp.float32
BF16 = jnp.bfloat16
MIB = 1024 * 1024
GROUP = 2
AHEAD = 3


def pack_stat(stat):
    high = stat.astype(BF16)
    rest = stat - high.astype(F32)
    mid = rest.astype(BF16)
    low = (rest - mid.astype(F32)).astype(BF16)
    return high, mid, low


def read_stat(ref):
    requests = ref.shape[0] - 1
    parts = [ref[requests, :, i * 128 : (i + 1) * 128].astype(F32) for i in range(3)]
    return parts[0] + parts[1] + parts[2]


def write_stat(ref, stat):
    requests = ref.shape[0] - 1
    for i, part in enumerate(pack_stat(stat)):
        ref[requests, :, i * 128 : (i + 1) * 128] = part
    used = 3 * 128
    if ref.shape[2] > used:
        ref[requests, :, used:] = jnp.zeros((ref.shape[1], ref.shape[2] - used), BF16)


def plan_kernel(split_count, block, dest_ref, len_ref, table_ref, split_ref, out_ref, next_ref):
    requests = dest_ref.shape[1]
    slots = table_ref.shape[3] // requests
    split = split_ref[0]
    counts = []
    for i in range(requests):
        total = lax.div(len_ref[0, i] + (block - 1), block)
        counts.append(lax.div(total - split + (split_count - 1), split_count))
    pairs = [lax.div(count + 1, 2) for count in counts]
    for c in range(slots // 2 + 1):
        shorter = [(p < c).astype(jnp.int32) for p in pairs]
        next_ref[c] = functools.reduce(jnp.add, shorter)
    for i in range(requests):
        at = next_ref[pairs[i]]
        next_ref[pairs[i]] = at + 1
        start = (counts[i] - 1) * split_count + split
        used = (counts[i] - 1) * block + jnp.minimum(block, len_ref[0, i] - start * block)
        out_ref[at, 0] = dest_ref[0, i]
        out_ref[at, 1] = pairs[i]
        out_ref[at, 2] = jnp.where(counts[i] > 0, used, 0)
        for j in range(slots):
            out_ref[at, 3 + j] = table_ref[0, 0, 0, i * slots + j]


def attention_kernel(n_pieces, plan_ref, *refs):
    q_refs = refs[:n_pieces]
    pool_ref = refs[n_pieces]
    o_refs = refs[n_pieces + 1 : 2 * n_pieces + 1]
    kbuf, stat_ref, sems = refs[2 * n_pieces + 1 :]
    requests, rows, _ = q_refs[0].shape
    slots = plan_ref.shape[1] - 3
    block = pool_ref.shape[2]
    latent = o_refs[0].shape[2]
    groups = requests // GROUP

    def fetch(g):
        pairs = plan_ref[g * GROUP + GROUP - 1, 1]
        part = lax.rem(g, AHEAD + 1)
        for c in range(slots // 2):

            @pl.when(c < pairs)
            def _():
                for m in range(GROUP):
                    for j in (2 * c, 2 * c + 1):
                        pltpu.make_async_copy(
                            pool_ref.at[plan_ref[g * GROUP + m, 3 + j]],
                            kbuf.at[part, m, j],
                            sems.at[part],
                        ).start()

    def arrived(part, pairs):
        blocks = kbuf.at[part, :, pl.ds(0, 2 * pairs)]
        pltpu.make_async_copy(blocks, blocks, sems.at[part]).wait()

    for g in range(AHEAD):
        fetch(g)
    stat_ref[...] = jnp.zeros_like(stat_ref)
    lane = lax.broadcasted_iota(jnp.int32, stat_ref.shape, 1)
    pair = 2 * block
    column = lax.broadcasted_iota(jnp.int32, (1, pair), 1)

    def compute(g, pairs):
        part = lax.rem(g, AHEAD + 1)
        arrived(part, pairs)
        whos = [plan_ref[g * GROUP + m, 0] for m in range(GROUP)]
        keys, scores, tops = [], [], []
        for m, who in enumerate(whos):
            used = plan_ref[g * GROUP + m, 2]
            q = jnp.concatenate([ref[who] for ref in q_refs], axis=0)
            keys.append(
                [
                    jnp.concatenate([kbuf[part, m, 2 * c], kbuf[part, m, 2 * c + 1]], axis=1)
                    for c in range(pairs)
                ]
            )
            row = []
            for c in range(pairs):
                s = jnp.dot(q, keys[m][c], preferred_element_type=F32) * score_scale
                row.append(jnp.where(column < used - c * pair, s, -jnp.inf))
            scores.append(row)
        for row in scores:
            top = functools.reduce(jnp.maximum, row)
            tops.append(jnp.maximum(jnp.max(top, axis=1, keepdims=True), EMPTY))
        for m, who in enumerate(whos):
            total, out = None, None
            for c in range(pairs):
                e = jnp.exp2(scores[m][c] - tops[m])
                total = e if total is None else total + e
                product = lax.dot_general(
                    e.astype(BF16),
                    keys[m][c][:latent],
                    (((1,), (1,)), ((), ())),
                    preferred_element_type=F32,
                )
                out = product if out is None else out + product
            total = jnp.sum(total, axis=1, keepdims=True)
            some = total > 0
            out = (out * jnp.where(some, 1.0 / total, 0.0)).astype(BF16)
            for n, ref in enumerate(o_refs):
                ref[who] = out[n * rows : (n + 1) * rows]
            stat = jnp.where(some, tops[m] + jnp.log2(total), EMPTY)
            stat_ref[...] = jnp.where(lane == who, stat, stat_ref[...])

    def step(g, carry):
        @pl.when(g + AHEAD < groups)
        def _():
            fetch(g + AHEAD)

        pairs_here = plan_ref[g * GROUP + GROUP - 1, 1]
        for pairs in range(1, slots // 2 + 1):

            @pl.when(pairs_here == pairs)
            def _():
                compute(g, pairs)

        @pl.when(pairs_here == 0)
        def _():
            for m in range(GROUP):
                who = plan_ref[g * GROUP + m, 0]
                for ref in o_refs:
                    ref[who] = jnp.zeros((rows, latent), BF16)
                stat_ref[...] = jnp.where(lane == who, EMPTY, stat_ref[...])

        return carry

    lax.fori_loop(0, groups, step, 0)
    for n, ref in enumerate(o_refs):
        write_stat(ref, stat_ref[n * rows : (n + 1) * rows, :])


def weights_of(refs, spans):
    stats = []
    for ref, (first, last) in zip(refs, spans):
        stat = read_stat(ref)
        lane = lax.broadcasted_iota(jnp.int32, stat.shape, 1)
        stats.append(jnp.where((lane >= first) & (lane < last), stat, EMPTY))
    top = functools.reduce(jnp.maximum, stats)
    parts = [jnp.exp2(stat - top) for stat in stats]
    total = functools.reduce(jnp.add, parts)
    share = 1.0 / total
    return [part * share for part in parts], top + jnp.log2(total)


def combined(refs, spans, weights, who):
    out = None
    for ref, (first, last), weight in zip(refs, spans, weights):
        if first <= who < last:
            part = ref[who - first].astype(F32) * weight[:, who : who + 1]
            out = part if out is None else out + part
    return out


def combine_kernel(spans, out_spans, *refs):
    pieces, out_refs = refs[: len(spans)], refs[len(spans) :]
    weights, stat = weights_of(pieces, spans)
    for out_ref, (first, last) in zip(out_refs, out_spans):
        write_stat(out_ref, stat)
        for who in range(first, last):
            out_ref[who - first] = combined(pieces, spans, weights, who).astype(BF16)


def project(latents, stats, proj_ref, out_ref):
    requests, steps, _ = out_ref.shape
    heads, _, width = proj_ref.shape
    latent = jnp.concatenate(latents, axis=0)
    stat = jnp.concatenate(stats, axis=0)
    shape = (latent.shape[0], width)
    head_of = lax.broadcasted_iota(jnp.int32, shape, 0) % heads

    def by_row(value):
        return value.reshape(requests * steps, heads, width).sum(axis=1)

    def put(value, at):
        for who in range(requests):
            out_ref[who, :, at : at + width] = value[who * steps : (who + 1) * steps]

    for h in range(heads):
        value = jnp.dot(latent, proj_ref[h], preferred_element_type=F32)
        put(by_row(jnp.where(head_of == h, value, 0.0)), h * width)
    lane = lax.broadcasted_iota(jnp.int32, shape, 1)
    put(by_row(jnp.where(head_of == lane, stat, 0.0)), heads * width)


def new_keys_kernel(q_ref, key_ref, proj_ref, out_ref):
    requests, rows, _ = q_ref.shape
    latent = proj_ref.shape[1]
    steps = key_ref.shape[1]
    heads = rows // steps
    step_of = lax.broadcasted_iota(jnp.int32, (rows, 1), 0) // heads
    latents, stats = [], []
    for who in range(requests):
        q = q_ref[who].astype(F32)
        keys = key_ref[who].astype(F32)
        scores = []
        for j in range(steps):
            s = jnp.sum(q * keys[j : j + 1, :], axis=1, keepdims=True) * score_scale
            scores.append(jnp.where(step_of >= j, s, -jnp.inf))
        top = functools.reduce(jnp.maximum, scores)
        parts = [jnp.exp2(s - top) for s in scores]
        total = functools.reduce(jnp.add, parts)
        out = None
        for j in range(steps):
            part = parts[j].astype(BF16).astype(F32) * keys[j : j + 1, :latent]
            out = part if out is None else out + part
        latents.append((out / total).astype(BF16))
        stats.append(top + jnp.log2(total))
    project(latents, stats, proj_ref, out_ref)


def finish_kernel(*refs):
    *pieces, proj_ref, out_ref = refs
    requests = out_ref.shape[0]
    spans = [(0, requests)] * len(pieces)
    weights, stat = weights_of(pieces, spans)
    latents = [
        combined(pieces, spans, weights, who).astype(BF16) for who in range(requests)
    ]
    stats = [stat[:, who : who + 1] for who in range(requests)]
    project(latents, stats, proj_ref, out_ref)


def merge_kernel(cache_ref, new_ref, out_ref):
    width = out_ref.shape[2]
    heads = width // 128
    cache_stat = cache_ref[:, :, width:]
    new_stat = new_ref[:, :, width:]
    top = jnp.maximum(cache_stat, new_stat)
    cache_part = jnp.exp2(cache_stat - top)
    new_part = jnp.exp2(new_stat - top)
    share = 1.0 / (cache_part + new_part)
    cache_part = cache_part * share
    new_part = new_part * share
    for h in range(heads):
        at = slice(h * 128, (h + 1) * 128)
        value = cache_ref[:, :, at] * cache_part[:, :, h : h + 1]
        value = value + new_ref[:, :, at] * new_part[:, :, h : h + 1]
        out_ref[:, :, at] = value.astype(BF16)


def call(kernel, out_shape, *args, mib=12, **extra):
    return pl.pallas_call(
        kernel,
        out_shape=out_shape,
        compiler_params=pltpu.CompilerParams(vmem_limit_bytes=mib * MIB),
        **extra,
    )(*args)


def vmem(count):
    return [pl.BlockSpec(memory_space=pltpu.VMEM)] * count


def smem(count):
    return [pl.BlockSpec(memory_space=pltpu.SMEM)] * count


def combine(pieces, out_spans):
    arrays = [array for array, _ in pieces]
    spans = tuple(span for _, span in pieces)
    shapes = [
        jax.ShapeDtypeStruct((last - first + 1,) + arrays[0].shape[1:], BF16)
        for first, last in out_spans
    ]
    outs = call(
        functools.partial(combine_kernel, spans, tuple(out_spans)),
        shapes,
        *arrays,
        in_specs=vmem(len(arrays)),
        out_specs=vmem(len(shapes)),
    )
    return list(zip(outs, out_spans))


def shards(block_pool, block_table, lengths, destination, query_latent, new_latent, value_proj):
    ring = lax.axis_size("seq")
    split_count = ring * lax.axis_size("dec")
    split_index = lax.axis_index(("seq", "dec"))
    requests = destination.shape[1]
    _, _, steps, heads, width = query_latent.shape
    rows = steps * heads
    latent, value_width = value_proj.shape[1:]
    block = block_pool.shape[4]
    slots = block_table.shape[3] // requests
    far, near = ring // 2, (ring - 1) // 2
    pool = jnp.swapaxes(block_pool[0, 0, 0], 1, 2)

    up = [(i, (i + 1) % ring) for i in range(ring)]
    down = [(i, (i - 1) % ring) for i in range(ring)]

    def swap(x):
        return lax.ppermute(x, "dec", [(0, 1), (1, 0)])

    decode_q = query_latent[0].reshape(requests, rows, width)
    own_q = lax.all_to_all(decode_q, "pre", split_axis=0, concat_axis=0, tiled=True)
    plan = call(
        functools.partial(plan_kernel, split_count, block),
        jax.ShapeDtypeStruct((requests, 3 + slots), jnp.int32),
        destination,
        lengths,
        block_table,
        split_index.reshape(1),
        in_specs=smem(4),
        out_specs=smem(1)[0],
        scratch_shapes=[pltpu.SMEM((slots // 2 + 1,), jnp.int32)],
    )
    values_shape = jax.ShapeDtypeStruct(
        (requests, steps, heads * value_width + 128), F32
    )
    new_values = call(
        new_keys_kernel,
        values_shape,
        decode_q,
        new_latent[0],
        value_proj,
        in_specs=vmem(3),
        out_specs=vmem(1)[0],
    )

    queries = {0: own_q}
    for s in range(1, far + 1):
        queries[-s] = lax.ppermute(queries[1 - s], "seq", up)
        if s <= near:
            queries[s] = lax.ppermute(queries[s - 1], "seq", down)
        if s == 1:
            queries[-s], plan = lax.optimization_barrier((queries[-s], plan))
        if s == 2:
            queries[-s], new_values = lax.optimization_barrier((queries[-s], new_values))
    order = sorted(queries)
    q_list = [queries[r] for r in order] + [swap(queries[r]) for r in order]
    n_pieces = len(q_list)
    piece = jax.ShapeDtypeStruct((requests + 1, rows, latent), BF16)
    outs = call(
        functools.partial(attention_kernel, n_pieces),
        [piece] * n_pieces,
        plan,
        *q_list,
        pool,
        in_specs=smem(1) + vmem(n_pieces) + [pl.BlockSpec(memory_space=pltpu.HBM)],
        out_specs=vmem(n_pieces),
        scratch_shapes=[
            pltpu.VMEM((AHEAD + 1, GROUP, slots, width, block), BF16),
            pltpu.VMEM((n_pieces * rows, 128), F32),
            pltpu.SemaphoreType.DMA((AHEAD + 1,)),
        ],
        mib=44,
    )
    everything = (0, requests)
    both = {
        r: [(own, everything), (swap(other), everything)]
        for r, own, other in zip(order, outs[: len(order)], outs[len(order) :])
    }

    def sent(piece, way):
        array, span = piece
        return [(lax.ppermute(array, "seq", way), span)]

    halves = [(0, requests // 2), (requests // 2, requests)]
    low, high = combine(both[-far], halves)
    from_up, from_down = sent(low, down), sent(high, up)
    for s in range(far - 1, 0, -1):
        from_up = sent(combine(both[-s] + from_up, [everything])[0], down)
        from_down = sent(combine(both[s] + from_down, [everything])[0], up)
    pieces = [array for array, _ in both[0] + from_up + from_down]
    values = call(
        finish_kernel,
        values_shape,
        *pieces,
        value_proj,
        in_specs=vmem(len(pieces) + 1),
        out_specs=vmem(1)[0],
    )
    got = lax.all_to_all(values, "pre", split_axis=0, concat_axis=0, tiled=True)
    result = call(
        merge_kernel,
        jax.ShapeDtypeStruct((requests, steps, heads * value_width), BF16),
        got,
        new_values,
        in_specs=vmem(2),
        out_specs=vmem(1)[0],
    )
    return result[None]


def solution(mesh):
    return jax.shard_map(
        shards,
        mesh=mesh,
        in_specs=(
            P("pre", "seq", "dec", None, None, None),
            P("pre", "seq", "dec", None),
            P("pre", None),
            P("pre", None),
            P("pre", None, None, ("seq", "dec"), None),
            P("pre", None, None, None),
            P(("seq", "dec"), None, None),
        ),
        out_specs=P("pre", None, None, ("seq", "dec")),
        check_vma=False,
    )
```

```python
import functools

import jax
import jax.numpy as jnp
from jax import lax
from jax.experimental import pallas as pl
from jax.experimental.pallas import tpu as pltpu
from jax.sharding import PartitionSpec as P

score_scale = 192.0 ** (-0.5) * 1.4426950408889634
EMPTY = -(2.0**127)
F32 = jnp.float32
BF16 = jnp.bfloat16
MIB = 1024 * 1024
GROUP = 2
AHEAD = 3


def pack_stat(stat):
    high = stat.astype(BF16)
    rest = stat - high.astype(F32)
    mid = rest.astype(BF16)
    low = (rest - mid.astype(F32)).astype(BF16)
    return high, mid, low


def read_stat(ref):
    requests = ref.shape[0] - 1
    parts = [ref[requests, :, i * 128 : (i + 1) * 128].astype(F32) for i in range(3)]
    return parts[0] + parts[1] + parts[2]


def write_stat(ref, stat):
    requests = ref.shape[0] - 1
    for i, part in enumerate(pack_stat(stat)):
        ref[requests, :, i * 128 : (i + 1) * 128] = part
    used = 3 * 128
    if ref.shape[2] > used:
        ref[requests, :, used:] = jnp.zeros((ref.shape[1], ref.shape[2] - used), BF16)


def plan_kernel(split_count, block, dest_ref, len_ref, table_ref, split_ref, out_ref, next_ref):
    requests = dest_ref.shape[1]
    slots = table_ref.shape[3] // requests
    split = split_ref[0]
    counts = []
    for i in range(requests):
        total = lax.div(len_ref[0, i] + (block - 1), block)
        counts.append(lax.div(total - split + (split_count - 1), split_count))
    pairs = [lax.div(count + 1, 2) for count in counts]
    for c in range(slots // 2 + 1):
        shorter = [(p < c).astype(jnp.int32) for p in pairs]
        next_ref[c] = functools.reduce(jnp.add, shorter)
    for i in range(requests):
        at = next_ref[pairs[i]]
        next_ref[pairs[i]] = at + 1
        start = (counts[i] - 1) * split_count + split
        used = (counts[i] - 1) * block + jnp.minimum(block, len_ref[0, i] - start * block)
        out_ref[at, 0] = dest_ref[0, i]
        out_ref[at, 1] = pairs[i]
        out_ref[at, 2] = jnp.where(counts[i] > 0, used, 0)
        for j in range(slots):
            out_ref[at, 3 + j] = table_ref[0, 0, 0, i * slots + j]


def attention_kernel(n_pieces, plan_ref, *refs):
    q_refs = refs[:n_pieces]
    pool_ref = refs[n_pieces]
    o_refs = refs[n_pieces + 1 : 2 * n_pieces + 1]
    kbuf, stat_ref, sems = refs[2 * n_pieces + 1 :]
    requests, rows, _ = q_refs[0].shape
    slots = plan_ref.shape[1] - 3
    block = pool_ref.shape[2]
    latent = o_refs[0].shape[2]
    groups = requests // GROUP

    def fetch(g):
        pairs = plan_ref[g * GROUP + GROUP - 1, 1]
        part = lax.rem(g, AHEAD + 1)
        for c in range(slots // 2):

            @pl.when(c < pairs)
            def _():
                for m in range(GROUP):
                    for j in (2 * c, 2 * c + 1):
                        pltpu.make_async_copy(
                            pool_ref.at[plan_ref[g * GROUP + m, 3 + j]],
                            kbuf.at[part, m, j],
                            sems.at[part],
                        ).start()

    def arrived(part, pairs):
        blocks = kbuf.at[part, :, pl.ds(0, 2 * pairs)]
        pltpu.make_async_copy(blocks, blocks, sems.at[part]).wait()

    for g in range(AHEAD):
        fetch(g)
    stat_ref[...] = jnp.zeros_like(stat_ref)
    lane = lax.broadcasted_iota(jnp.int32, stat_ref.shape, 1)
    pair = 2 * block
    column = lax.broadcasted_iota(jnp.int32, (1, pair), 1)

    def compute(g, pairs):
        part = lax.rem(g, AHEAD + 1)
        arrived(part, pairs)
        whos = [plan_ref[g * GROUP + m, 0] for m in range(GROUP)]
        keys, scores, tops = [], [], []
        for m, who in enumerate(whos):
            used = plan_ref[g * GROUP + m, 2]
            q = jnp.concatenate([ref[who] for ref in q_refs], axis=0)
            keys.append(
                [
                    jnp.concatenate([kbuf[part, m, 2 * c], kbuf[part, m, 2 * c + 1]], axis=1)
                    for c in range(pairs)
                ]
            )
            row = []
            for c in range(pairs):
                s = jnp.dot(q, keys[m][c], preferred_element_type=F32) * score_scale
                row.append(jnp.where(column < used - c * pair, s, -jnp.inf))
            scores.append(row)
        for row in scores:
            top = functools.reduce(jnp.maximum, row)
            tops.append(jnp.maximum(jnp.max(top, axis=1, keepdims=True), EMPTY))
        for m, who in enumerate(whos):
            total, out = None, None
            for c in range(pairs):
                e = jnp.exp2(scores[m][c] - tops[m])
                total = e if total is None else total + e
                product = lax.dot_general(
                    e.astype(BF16),
                    keys[m][c][:latent],
                    (((1,), (1,)), ((), ())),
                    preferred_element_type=F32,
                )
                out = product if out is None else out + product
            total = jnp.sum(total, axis=1, keepdims=True)
            some = total > 0
            out = (out * jnp.where(some, 1.0 / total, 0.0)).astype(BF16)
            for n, ref in enumerate(o_refs):
                ref[who] = out[n * rows : (n + 1) * rows]
            stat = jnp.where(some, tops[m] + jnp.log2(total), EMPTY)
            stat_ref[...] = jnp.where(lane == who, stat, stat_ref[...])

    def step(g, carry):
        @pl.when(g + AHEAD < groups)
        def _():
            fetch(g + AHEAD)

        pairs_here = plan_ref[g * GROUP + GROUP - 1, 1]
        for pairs in range(1, slots // 2 + 1):

            @pl.when(pairs_here == pairs)
            def _():
                compute(g, pairs)

        @pl.when(pairs_here == 0)
        def _():
            for m in range(GROUP):
                who = plan_ref[g * GROUP + m, 0]
                for ref in o_refs:
                    ref[who] = jnp.zeros((rows, latent), BF16)
                stat_ref[...] = jnp.where(lane == who, EMPTY, stat_ref[...])

        return carry

    lax.fori_loop(0, groups, step, 0)
    for n, ref in enumerate(o_refs):
        write_stat(ref, stat_ref[n * rows : (n + 1) * rows, :])


def weights_of(refs, spans):
    stats = []
    for ref, (first, last) in zip(refs, spans):
        stat = read_stat(ref)
        lane = lax.broadcasted_iota(jnp.int32, stat.shape, 1)
        stats.append(jnp.where((lane >= first) & (lane < last), stat, EMPTY))
    top = functools.reduce(jnp.maximum, stats)
    parts = [jnp.exp2(stat - top) for stat in stats]
    total = functools.reduce(jnp.add, parts)
    share = 1.0 / total
    return [part * share for part in parts], top + jnp.log2(total)


def combined(refs, spans, weights, who):
    out = None
    for ref, (first, last), weight in zip(refs, spans, weights):
        if first <= who < last:
            part = ref[who - first].astype(F32) * weight[:, who : who + 1]
            out = part if out is None else out + part
    return out


def combine_kernel(spans, out_spans, *refs):
    pieces, out_refs = refs[: len(spans)], refs[len(spans) :]
    weights, stat = weights_of(pieces, spans)
    for out_ref, (first, last) in zip(out_refs, out_spans):
        write_stat(out_ref, stat)
        for who in range(first, last):
            out_ref[who - first] = combined(pieces, spans, weights, who).astype(BF16)


def project(latents, stats, proj_ref, out_ref):
    requests, steps, _ = out_ref.shape
    heads, _, width = proj_ref.shape
    latent = jnp.concatenate(latents, axis=0)
    stat = jnp.concatenate(stats, axis=0)
    shape = (latent.shape[0], width)
    head_of = lax.broadcasted_iota(jnp.int32, shape, 0) % heads

    def by_row(value):
        return value.reshape(requests * steps, heads, width).sum(axis=1)

    def put(value, at):
        for who in range(requests):
            out_ref[who, :, at : at + width] = value[who * steps : (who + 1) * steps]

    for h in range(heads):
        value = jnp.dot(latent, proj_ref[h], preferred_element_type=F32)
        put(by_row(jnp.where(head_of == h, value, 0.0)), h * width)
    lane = lax.broadcasted_iota(jnp.int32, shape, 1)
    put(by_row(jnp.where(head_of == lane, stat, 0.0)), heads * width)


def new_keys_kernel(q_ref, key_ref, proj_ref, out_ref):
    requests, rows, _ = q_ref.shape
    latent = proj_ref.shape[1]
    steps = key_ref.shape[1]
    heads = rows // steps
    step_of = lax.broadcasted_iota(jnp.int32, (rows, 1), 0) // heads
    latents, stats = [], []
    for who in range(requests):
        q = q_ref[who].astype(F32)
        keys = key_ref[who].astype(F32)
        scores = []
        for j in range(steps):
            s = jnp.sum(q * keys[j : j + 1, :], axis=1, keepdims=True) * score_scale
            scores.append(jnp.where(step_of >= j, s, -jnp.inf))
        top = functools.reduce(jnp.maximum, scores)
        parts = [jnp.exp2(s - top) for s in scores]
        total = functools.reduce(jnp.add, parts)
        out = None
        for j in range(steps):
            part = parts[j].astype(BF16).astype(F32) * keys[j : j + 1, :latent]
            out = part if out is None else out + part
        latents.append((out / total).astype(BF16))
        stats.append(top + jnp.log2(total))
    project(latents, stats, proj_ref, out_ref)


def finish_kernel(*refs):
    *pieces, proj_ref, out_ref = refs
    requests = out_ref.shape[0]
    spans = [(0, requests)] * len(pieces)
    weights, stat = weights_of(pieces, spans)
    latents = [
        combined(pieces, spans, weights, who).astype(BF16) for who in range(requests)
    ]
    stats = [stat[:, who : who + 1] for who in range(requests)]
    project(latents, stats, proj_ref, out_ref)


def merge_kernel(cache_ref, new_ref, out_ref):
    width = out_ref.shape[2]
    heads = width // 128
    cache_stat = cache_ref[:, :, width:]
    new_stat = new_ref[:, :, width:]
    top = jnp.maximum(cache_stat, new_stat)
    cache_part = jnp.exp2(cache_stat - top)
    new_part = jnp.exp2(new_stat - top)
    share = 1.0 / (cache_part + new_part)
    cache_part = cache_part * share
    new_part = new_part * share
    for h in range(heads):
        at = slice(h * 128, (h + 1) * 128)
        value = cache_ref[:, :, at] * cache_part[:, :, h : h + 1]
        value = value + new_ref[:, :, at] * new_part[:, :, h : h + 1]
        out_ref[:, :, at] = value.astype(BF16)


def call(kernel, out_shape, *args, mib=12, **extra):
    return pl.pallas_call(
        kernel,
        out_shape=out_shape,
        compiler_params=pltpu.CompilerParams(vmem_limit_bytes=mib * MIB),
        **extra,
    )(*args)


def vmem(count):
    return [pl.BlockSpec(memory_space=pltpu.VMEM)] * count


def smem(count):
    return [pl.BlockSpec(memory_space=pltpu.SMEM)] * count


def combine(pieces, out_spans):
    arrays = [array for array, _ in pieces]
    spans = tuple(span for _, span in pieces)
    shapes = [
        jax.ShapeDtypeStruct((last - first + 1,) + arrays[0].shape[1:], BF16)
        for first, last in out_spans
    ]
    outs = call(
        functools.partial(combine_kernel, spans, tuple(out_spans)),
        shapes,
        *arrays,
        in_specs=vmem(len(arrays)),
        out_specs=vmem(len(shapes)),
    )
    return list(zip(outs, out_spans))


def shards(block_pool, block_table, lengths, destination, query_latent, new_latent, value_proj):
    ring = lax.axis_size("seq")
    split_count = ring * lax.axis_size("dec")
    split_index = lax.axis_index(("seq", "dec"))
    requests = destination.shape[1]
    _, _, steps, heads, width = query_latent.shape
    rows = steps * heads
    latent, value_width = value_proj.shape[1:]
    block = block_pool.shape[4]
    slots = block_table.shape[3] // requests
    far, near = ring // 2, (ring - 1) // 2
    pool = jnp.swapaxes(block_pool[0, 0, 0], 1, 2)

    up = [(i, (i + 1) % ring) for i in range(ring)]
    down = [(i, (i - 1) % ring) for i in range(ring)]

    def swap(x):
        return lax.ppermute(x, "dec", [(0, 1), (1, 0)])

    decode_q = query_latent[0].reshape(requests, rows, width)
    own_q = lax.all_to_all(decode_q, "pre", split_axis=0, concat_axis=0, tiled=True)
    plan = call(
        functools.partial(plan_kernel, split_count, block),
        jax.ShapeDtypeStruct((requests, 3 + slots), jnp.int32),
        destination,
        lengths,
        block_table,
        split_index.reshape(1),
        in_specs=smem(4),
        out_specs=smem(1)[0],
        scratch_shapes=[pltpu.SMEM((slots // 2 + 1,), jnp.int32)],
    )
    values_shape = jax.ShapeDtypeStruct(
        (requests, steps, heads * value_width + 128), F32
    )
    new_values = call(
        new_keys_kernel,
        values_shape,
        decode_q,
        new_latent[0],
        value_proj,
        in_specs=vmem(3),
        out_specs=vmem(1)[0],
    )

    queries = {0: own_q}
    for s in range(1, far + 1):
        queries[-s] = lax.ppermute(queries[1 - s], "seq", up)
        if s <= near:
            queries[s] = lax.ppermute(queries[s - 1], "seq", down)
        if s == 1:
            queries[-s], plan = lax.optimization_barrier((queries[-s], plan))
        if s == 2:
            queries[-s], new_values = lax.optimization_barrier((queries[-s], new_values))
    order = sorted(queries)
    q_list = [queries[r] for r in order] + [swap(queries[r]) for r in order]
    n_pieces = len(q_list)
    piece = jax.ShapeDtypeStruct((requests + 1, rows, latent), BF16)
    outs = call(
        functools.partial(attention_kernel, n_pieces),
        [piece] * n_pieces,
        plan,
        *q_list,
        pool,
        in_specs=smem(1) + vmem(n_pieces) + [pl.BlockSpec(memory_space=pltpu.HBM)],
        out_specs=vmem(n_pieces),
        scratch_shapes=[
            pltpu.VMEM((AHEAD + 1, GROUP, slots, width, block), BF16),
            pltpu.VMEM((n_pieces * rows, 128), F32),
            pltpu.SemaphoreType.DMA((AHEAD + 1,)),
        ],
        mib=44,
    )
    everything = (0, requests)
    both = {
        r: [(own, everything), (swap(other), everything)]
        for r, own, other in zip(order, outs[: len(order)], outs[len(order) :])
    }

    def sent(piece, way):
        array, span = piece
        return [(lax.ppermute(array, "seq", way), span)]

    cut = requests * 5 // 8
    halves = [(0, cut), (cut, requests)]
    low, high = combine(both[-far], halves)
    from_up, from_down = sent(low, down), sent(high, up)
    for s in range(far - 1, 0, -1):
        from_up = sent(combine(both[-s] + from_up, [everything])[0], down)
        from_down = sent(combine(both[s] + from_down, [everything])[0], up)
    pieces = [array for array, _ in both[0] + from_up + from_down]
    values = call(
        finish_kernel,
        values_shape,
        *pieces,
        value_proj,
        in_specs=vmem(len(pieces) + 1),
        out_specs=vmem(1)[0],
    )
    got = lax.all_to_all(values, "pre", split_axis=0, concat_axis=0, tiled=True)
    result = call(
        merge_kernel,
        jax.ShapeDtypeStruct((requests, steps, heads * value_width), BF16),
        got,
        new_values,
        in_specs=vmem(2),
        out_specs=vmem(1)[0],
    )
    return result[None]


def solution(mesh):
    return jax.shard_map(
        shards,
        mesh=mesh,
        in_specs=(
            P("pre", "seq", "dec", None, None, None),
            P("pre", "seq", "dec", None),
            P("pre", None),
            P("pre", None),
            P("pre", None, None, ("seq", "dec"), None),
            P("pre", None, None, None),
            P(("seq", "dec"), None, None),
        ),
        out_specs=P("pre", None, None, ("seq", "dec")),
        check_vma=False,
    )
```
